256 devices in a mesh: group: 64 (over z, x, core), head: 4 (over y).
Axes of the slice: x: 4, y: 4, z: 8, core: 2. Of those that a mesh axis runs over, the one named last changes fastest.
Arguments:
- hidden: bfloat16 [16384, 3072], P(('group', 'head')), may hold values from -4 to 4
- query: bfloat16 [16384, 1536], P(('group', 'head')), may hold values from -128 to 128
- keys: bfloat16 [16384, 1536], P(('group', 'head')), may hold values from -4 to 4
- values: bfloat16 [16384, 1536], P(('group', 'head')), may hold values from -6 to 6
- attends: int32 [64, 64], P('group'), may hold values from 0 to 1, as said below
- levels: int32 [64], P('group'), may hold values from 0 to 63
- out_weight: bfloat16 [1536, 3072], P('head'), may hold values from -1.25 to 1.25
- gate_table: float32 [64, 3072], replicated, may hold values from -6 to 6
Outputs:
- updated: bfloat16 [16384, 3072], P(('group', 'head'))
The draws below stay inside these ranges and needn't reach their ends.
Inputs may be any that keep to these rules, and one draw needn't show every extreme that they name: attends[c, c] is 1 and attends[c, j] is 0 for j > c; how many earlier groups a group attends to differs from group to group.
All inputs are finite; a program needn't handle non-finite values.
Results may differ from the reference program's by a relative error of at most 0.017.
Values may be sent and summed in bfloat16 or wider, within the bound.
A program may use at most 192 MiB of HBM per device.

```python
import jax
import jax.numpy as jnp
from jax import lax

D = 3072
HEADS = 12
HS = 128
CT = 256
LEVELS = 64
GROUPS = 64
TOKENS = 16384
N_GROUP = 64


def shared_keys(key):
    return jnp.clip(jax.random.normal(key, (TOKENS, HEADS * HS), jnp.float32), -4.0, 4.0)


def draw_keys(key, part):
    shared_base = shared_keys(key)
    return shared_base.astype(jnp.bfloat16)


def draw_query(key, part):
    key = jax.random.fold_in(key, 33)
    drawn_query = 2.0 * jnp.clip(jax.random.normal(key, (TOKENS, HEADS * HS), jnp.float32), -4.0, 4.0)
    return drawn_query.astype(jnp.bfloat16)


def draw_attends(key, part):
    key = jax.random.fold_in(key, 7)
    first_key, second_key = jax.random.split(key)
    keep_rate = jax.random.randint(first_key, (GROUPS, 1), 1, 5)
    rolled = jax.random.randint(second_key, (GROUPS, GROUPS), 0, 4)
    positions = jnp.arange(GROUPS)
    earlier = positions[None, :] < positions[:, None]
    itself = positions[None, :] == positions[:, None]
    chosen = earlier & (rolled < keep_rate) | itself
    return chosen.astype(jnp.int32)


def with_ends(values, rng, low, largest):
    extent = values.shape
    index_at = [jax.random.randint(jax.random.fold_in(rng, axis), (), 0, extent[axis]) for axis in range(len(extent))]
    values = values.at[tuple(index_at)].set(low)
    longest = extent.index(max(extent))
    index_at[longest] = (index_at[longest] + 1) % extent[longest]
    return values.at[tuple(index_at)].set(largest)


def level_of(own_key, dims, pieces, smallest, high):
    factor_of = 1.0
    for axis_at, parts in pieces:
        draws = jax.random.uniform(jax.random.fold_in(jax.random.fold_in(own_key, 6), axis_at), (parts,), jnp.float32, smallest / len(pieces), high / len(pieces))
        factor_of = factor_of * jnp.repeat(jnp.exp(draws), dims[axis_at] // parts).reshape((-1,) + (1,) * (len(dims) - 1 - axis_at))
    return factor_of


def bell_draw(stream_key, dims, width, reach, pieces=(), dtype=jnp.bfloat16):
    loudness = level_of(stream_key, dims, pieces, -0.22, 0.18) if pieces else 1.0
    drawn = jax.random.normal(stream_key, dims, jnp.float32) * width * loudness
    return jnp.minimum(jnp.maximum(drawn, -reach), reach).astype(dtype)


def setup_inputs(seed: int = 0) -> dict:
    streams_of = jax.random.split(jax.random.key(seed), 9)
    hidden = bell_draw(streams_of[0], (TOKENS, D), 0.25, 4.0, ((0, 256),))
    query = draw_query(jax.random.fold_in(streams_of[8], 71), 0)
    keys = draw_keys(jax.random.fold_in(streams_of[8], 71), 0)
    values = bell_draw(streams_of[3], (TOKENS, HEADS * HS), 1.0, 6.0, ((0, 256),))
    attends = draw_attends(jax.random.fold_in(streams_of[8], 71), 0)
    levels = with_ends(jax.random.randint(streams_of[5], (GROUPS,), 0, LEVELS), jax.random.fold_in(streams_of[5], 1), 0, LEVELS - 1).astype(jnp.int32)
    out_weight = bell_draw(streams_of[6], (HEADS * HS, D), (HEADS * HS // 64) ** -0.5, 1.25, ((0, 4),))
    gate_table = bell_draw(streams_of[7], (LEVELS, D), 1.5, 6.0, (), jnp.float32)
    return {"hidden": hidden, "query": query, "keys": keys, "values": values, "attends": attends, "levels": levels, "out_weight": out_weight, "gate_table": gate_table}


def group_attention(query_block, mask_row, keys_all, values_all):
    scores = jnp.einsum("qhd,khd->hqk", query_block.astype(jnp.float32), keys_all)
    scores = scores * (HS ** -0.5)
    visible = jnp.repeat(mask_row, CT, total_repeat_length=N_GROUP * CT) > 0
    scores = jnp.where(visible[None, None, :], scores, -1e30)
    highest = jnp.max(scores, axis=-1, keepdims=True)
    weights = jnp.where(visible[None, None, :], jnp.exp(scores - highest), 0.0)
    totals = jnp.sum(weights, axis=-1)
    rounded = lax.optimization_barrier(weights.astype(jnp.bfloat16)).astype(jnp.float32)
    summed = jnp.einsum("hqk,khd->qhd", rounded, values_all)
    result = summed / jnp.transpose(totals)[:, :, None]
    return result.astype(jnp.bfloat16).reshape(CT, HEADS * HS)


def reference(hidden, query, keys, values, attends, levels, out_weight, gate_table):
    query_blocks = query.reshape(N_GROUP, CT, HEADS, HS)
    keys_all = keys.astype(jnp.float32).reshape(N_GROUP * CT, HEADS, HS)
    values_all = values.astype(jnp.float32).reshape(N_GROUP * CT, HEADS, HS)

    def one_group(paired):
        return group_attention(paired[0], paired[1], keys_all, values_all)

    attended = lax.map(one_group, (query_blocks, attends))
    attended = attended.reshape(N_GROUP * CT, HEADS * HS)
    projected = jnp.dot(attended, out_weight, preferred_element_type=jnp.float32)
    gates = jnp.repeat(gate_table[levels], CT, axis=0)
    return (hidden.astype(jnp.float32) + gates * projected).astype(jnp.bfloat16)
```

```python
import functools

import jax
import jax.numpy as jnp
from jax import lax
from jax.experimental import pallas as pl
from jax.experimental.pallas import tpu as pltpu
from jax.sharding import Mesh, PartitionSpec as P

HS = 128
NZ, NX, NC, NY = 8, 4, 2, 4
GROUPS = 64
ROWS = 256
PART = 64
WIDTH = 384
HEADS = WIDTH // HS
D = 3072
SCALE = 1.4426950408889634 * HS**-0.5
NONE = -1e30
MESH_ID = pl.DeviceIdType.MESH


def attention_kernel(
    q_hbm, k_hbm, v_hbm, bias_in, out_hbm,
    qin, vin, kbuf, vbuf, qt, bias, acc, top, total, osend, orecv, ssend, srecv, att,
    loc_sem, a2a_send, a2a_recv, bias_send, bias_recv, q_send, q_recv,
    up_send, dn_send, z_recv, sib_send, sib_recv,
    o_send, o_recv, s_send, s_recv, y_send, y_recv,
):
    z, x, c, y = (lax.axis_index(a) for a in ("z", "x", "c", "head"))
    above, below = (z + 1) % NZ, (z + NZ - 1) % NZ

    def remote(src, dst, send, recv, dz=None, dx=None, dc=None, dy=None):
        return pltpu.make_async_remote_copy(
            src_ref=src, dst_ref=dst, send_sem=send, recv_sem=recv,
            device_id=(
                z if dz is None else dz, x if dx is None else dx,
                c if dc is None else dc, y if dy is None else dy,
            ),
            device_id_type=MESH_ID,
        )

    barrier = pltpu.get_barrier_semaphore()
    peers = [(z, x, c, (y + d) % NY) for d in range(1, NY)]
    peers += [(z, (x + d) % NX, c, y) for d in range(1, NX)]
    peers += [(z, x, 1 - c, y), (above, x, c, y), (below, x, c, y)]
    for peer in peers:
        pl.semaphore_signal(barrier, inc=1, device_id=peer, device_id_type=MESH_ID)
    pl.semaphore_wait(barrier, len(peers))

    own_rows = pl.ds(pl.multiple_of(y * PART, PART), PART)

    def columns(owner):
        return pl.ds(pl.multiple_of(owner * WIDTH, WIDTH), WIDTH)

    landing = [kbuf.at[z, c], vin, qin]
    sources = [k_hbm, v_hbm, q_hbm]

    def token_copy(a, d):
        dest = (y + d) % NY
        return remote(
            sources[a].at[:, columns(dest)], landing[a].at[own_rows, :],
            a2a_send.at[a, d - 1], a2a_recv.at[a, d - 1], dy=dest,
        )

    def own_copy(a):
        return pltpu.make_async_copy(
            sources[a].at[:, columns(y)], landing[a].at[own_rows, :], loc_sem.at[a]
        )

    for a in range(3):
        for d in range(1, NY):
            token_copy(a, d).start()
        own_copy(a).start()

    def bias_copy(d):
        return remote(
            bias_in, bias.at[x], bias_send.at[d - 1], bias_recv.at[d - 1], dx=(x + d) % NX
        )

    for d in range(1, NX):
        bias_copy(d).start()
    bias[x] = bias_in[...]

    def token_wait(a):
        own_copy(a).wait()
        for d in range(1, NY):
            token_copy(a, d).wait_recv()

    bufs = [kbuf, vbuf]

    def block(kv, b, side):
        return bufs[kv].at[b, side]

    def up_copy(kv, b):
        return remote(block(kv, b, c), block(kv, b, c), up_send.at[kv, b], z_recv.at[kv, b], dz=above)

    def down_copy(kv, b):
        return remote(block(kv, b, c), block(kv, b, c), dn_send.at[kv, b], z_recv.at[kv, b], dz=below)

    def side_copy(kv, b, side):
        return remote(
            block(kv, b, side), block(kv, b, side), sib_send.at[kv, b], sib_recv.at[kv, b], dc=1 - c
        )

    def reaches_up(b, plane):
        return (plane < NZ) & ((plane - b <= 3) | (plane == NZ - 1) & (plane - b <= 4))

    def reaches_down(b, plane):
        return (b <= 2) & ((plane >= b + 4) | (plane < b))

    def forward(kv, b, up, down, side):
        @pl.when(side)
        def _():
            side_copy(kv, b, c).start()

        @pl.when(up)
        def _():
            up_copy(kv, b).start()

        @pl.when(down)
        def _():
            down_copy(kv, b).start()

    def finish(kv, b, up, down, side):
        @pl.when(side)
        def _():
            side_copy(kv, b, c).wait_send()

        @pl.when(up)
        def _():
            up_copy(kv, b).wait_send()

        @pl.when(down)
        def _():
            down_copy(kv, b).wait_send()

    own_plan = (z < NZ - 1, z <= 2, z >= 0)

    def rising(step):
        b = z - step
        here = (b >= 0) & reaches_up(jnp.maximum(b, 0), z)
        b = jnp.maximum(b, 0)
        return here, b, (here & reaches_up(b, z + 1), False, here)

    def falling(step):
        b = (z + step) % NZ
        here = reaches_down(b, z)
        return here, b, (False, here & reaches_down(b, below), here & (b < z))

    token_wait(0)
    forward(0, z, *own_plan)
    token_wait(1)
    for h in range(HEADS):
        vbuf[z, c, h * HS : (h + 1) * HS, :] = vin[:, h * HS : (h + 1) * HS].T
    forward(1, z, *own_plan)
    token_wait(2)
    for h in range(HEADS):
        qt[x, h * HS : (h + 1) * HS, :] = qin[:, h * HS : (h + 1) * HS].T

    def query_copy(d):
        return remote(qt.at[x], qt.at[x], q_send.at[d - 1], q_recv.at[d - 1], dx=(x + d) % NX)

    for d in range(1, NX):
        query_copy(d).start()

    acc[...] = jnp.zeros_like(acc)
    top[...] = jnp.full_like(top, NONE)
    total[...] = jnp.zeros_like(total)

    def query_wait(d):
        remote(
            qt.at[(x + NX - d) % NX], qt.at[(x + NX - d) % NX],
            q_send.at[d - 1], q_recv.at[d - 1], dx=(x + d) % NX,
        ).wait_recv()
        behind = bias.at[(x + NX - d) % NX]
        remote(
            behind, behind, bias_send.at[d - 1], bias_recv.at[d - 1], dx=(x + d) % NX
        ).wait_recv()

    def attend(b, r):
        group = b * (NX * NC) + x * NC
        offs = []
        for s in range(NC):
            row = bias[r, pl.ds(group + s, 1), :]
            offs.append(jnp.concatenate([row, row], axis=1))
        for h in range(HEADS):
            span = slice(h * HS, (h + 1) * HS)
            query = qt[r, span, :]
            scores = [
                jnp.dot(kbuf[b, s, :, span], query, preferred_element_type=jnp.float32)
                for s in range(NC)
            ]
            old = top[r, h : h + 1, :]
            new = old
            for s in range(NC):
                new = jnp.maximum(new, jnp.max(scores[s], axis=0, keepdims=True) + offs[s])
            factor = jnp.exp2((old - new) * SCALE)
            weights = [jnp.exp2(scores[s] * SCALE + (offs[s] - new * SCALE)) for s in range(NC)]
            sums = sum(jnp.sum(w, axis=0, keepdims=True) for w in weights)
            total[r, h : h + 1, :] = total[r, h : h + 1, :] * factor + sums
            top[r, h : h + 1, :] = new
            added = sum(
                jnp.dot(
                    vbuf[b, s, span, :], weights[s].astype(jnp.bfloat16),
                    preferred_element_type=jnp.float32,
                )
                for s in range(NC)
            )
            acc[r, span, :] = acc[r, span, :] * factor + added

    def attend_block(b, first):
        if first:
            attend(b, x)
            for d in range(1, NX):
                query_wait(d)
                attend(b, (x + NX - d) % NX)
        else:
            @pl.loop(0, NX)
            def _(r):
                attend(b, r)

    def receive(step):
        for plan in (rising, falling):
            here, b, moves = plan(step)

            @pl.when(here)
            def _():
                for kv in range(2):
                    up_copy(kv, b).wait_recv()
                    forward(kv, b, *moves)

    def side_wait(b):
        for kv in range(2):
            side_copy(kv, b, 1 - c).wait_recv()

    def compute(step):
        for plan in (rising, falling):
            here, b, moves = plan(step)

            @pl.when(moves[2])
            def _():
                side_wait(b)
                attend_block(b, False)

    receive(1)
    side_wait(z)
    attend_block(z, True)

    @pl.loop(2, 5)
    def _(step):
        receive(step)
        compute(step - 1)

    compute(4)

    def result_copy(d):
        return remote(
            osend.at[d - 1], orecv.at[d - 1], o_send.at[d - 1], o_recv.at[d - 1], dx=(x + d) % NX
        )

    def stats_copy(d):
        return remote(
            ssend.at[d - 1], srecv.at[d - 1], s_send.at[d - 1], s_recv.at[d - 1], dx=(x + d) % NX
        )

    for d in range(1, NX):
        r = (x + d) % NX
        ssend[d - 1, 0] = top[r]
        ssend[d - 1, 1] = total[r]
        stats_copy(d).start()
        osend[d - 1] = acc[r].astype(jnp.bfloat16)
        result_copy(d).start()

    for d in range(1, NX):
        stats_copy(d).wait_recv()
        result_copy(d).wait_recv()

    for h in range(HEADS):
        span = slice(h * HS, (h + 1) * HS)
        tops = [top[x, h : h + 1, :]] + [srecv[d, 0, h : h + 1, :] for d in range(NX - 1)]
        totals = [total[x, h : h + 1, :]] + [srecv[d, 1, h : h + 1, :] for d in range(NX - 1)]
        best = functools.reduce(jnp.maximum, tops)
        shares = [jnp.exp2((t - best) * SCALE) for t in tops]
        inverse = 1.0 / sum(s * t for s, t in zip(shares, totals))
        parts = [acc[x, span, :]] + [orecv[d, span, :].astype(jnp.float32) for d in range(NX - 1)]
        merged = sum(p * (s * inverse) for p, s in zip(parts, shares))
        att[:, span] = merged.astype(jnp.bfloat16).T

    def back_copy(d):
        dest = (y + d) % NY
        return remote(
            att.at[pl.ds(pl.multiple_of(dest * PART, PART), PART), :], out_hbm.at[:, columns(y)],
            y_send.at[d - 1], y_recv.at[d - 1], dy=dest,
        )

    keep = pltpu.make_async_copy(att.at[own_rows, :], out_hbm.at[:, columns(y)], loc_sem.at[0])
    for d in range(1, NY):
        back_copy(d).start()
    keep.start()

    for a in range(3):
        for d in range(1, NY):
            token_copy(a, d).wait_send()
    for d in range(1, NX):
        bias_copy(d).wait_send()
        query_copy(d).wait_send()
        result_copy(d).wait_send()
        stats_copy(d).wait_send()
    for kv in range(2):
        finish(kv, z, *own_plan)

    @pl.loop(1, 5)
    def _(step):
        for plan in (rising, falling):
            _, b, moves = plan(step)
            for kv in range(2):
                finish(kv, b, *moves)

    keep.wait()
    for d in range(1, NY):
        back_copy(d).wait()


def attention(query, keys, values, bias):
    dma = pltpu.SemaphoreType.DMA
    bf16, f32 = jnp.bfloat16, jnp.float32
    anywhere = pl.BlockSpec(memory_space=pl.ANY)
    return pl.pallas_call(
        attention_kernel,
        out_shape=jax.ShapeDtypeStruct((PART, NY * WIDTH), bf16),
        in_specs=[anywhere, anywhere, anywhere, pl.BlockSpec(memory_space=pltpu.VMEM)],
        out_specs=anywhere,
        scratch_shapes=[
            pltpu.VMEM((ROWS, WIDTH), bf16),
            pltpu.VMEM((ROWS, WIDTH), bf16),
            pltpu.VMEM((NZ, NC, ROWS, WIDTH), bf16),
            pltpu.VMEM((NZ, NC, WIDTH, ROWS), bf16),
            pltpu.VMEM((NX, WIDTH, ROWS), bf16),
            pltpu.VMEM((NX, GROUPS, HS), f32),
            pltpu.VMEM((NX, WIDTH, ROWS), f32),
            pltpu.VMEM((NX, 8, ROWS), f32),
            pltpu.VMEM((NX, 8, ROWS), f32),
            pltpu.VMEM((NX - 1, WIDTH, ROWS), bf16),
            pltpu.VMEM((NX - 1, WIDTH, ROWS), bf16),
            pltpu.VMEM((NX - 1, 2, 8, ROWS), f32),
            pltpu.VMEM((NX - 1, 2, 8, ROWS), f32),
            pltpu.VMEM((ROWS, WIDTH), bf16),
            dma((3,)), dma((3, NY - 1)), dma((3, NY - 1)),
            dma((NX - 1,)), dma((NX - 1,)), dma((NX - 1,)), dma((NX - 1,)),
            dma((2, NZ)), dma((2, NZ)), dma((2, NZ)), dma((2, NZ)), dma((2, NZ)),
            dma((NX - 1,)), dma((NX - 1,)), dma((NX - 1,)), dma((NX - 1,)),
            dma((NY - 1,)), dma((NY - 1,)),
        ],
        compiler_params=pltpu.CompilerParams(
            collective_id=0, has_side_effects=True, vmem_limit_bytes=40 * 1024 * 1024
        ),
        cost_estimate=pl.CostEstimate(
            flops=192 * 4 * ROWS * ROWS * HS, bytes_accessed=2**22, transcendentals=192 * ROWS * ROWS
        ),
    )(query, keys, values, bias)


def shards(hidden, query, keys, values, attends, levels, out_weight, gate_table):
    half = D // NC
    mine = lax.dynamic_slice_in_dim(out_weight, lax.axis_index("c") * half, half, axis=1)
    gathered = lax.all_gather(mine, ("c", "head"), axis=0, tiled=True)
    gathered = gathered.reshape(NC, NY * WIDTH, half)
    bias = jnp.where(attends[0] > 0, 0.0, NONE).astype(jnp.float32)
    bias = jnp.broadcast_to(bias[:, None], (GROUPS, HS))
    attended = attention(query, keys, values, bias)
    projected = jnp.concatenate(
        [jnp.dot(attended, gathered[s], preferred_element_type=jnp.float32) for s in range(NC)],
        axis=1,
    )
    gate_row = lax.dynamic_index_in_dim(gate_table, levels[0], 0, keepdims=True)
    return (hidden.astype(jnp.float32) + gate_row * projected).astype(jnp.bfloat16)


def solution(mesh):
    fine = Mesh(mesh.devices.reshape(NZ, NX, NC, NY), ("z", "x", "c", "head"))
    tokens = P(("z", "x", "c", "head"), None)
    group = ("z", "x", "c")
    placed = (
        tokens, tokens, tokens, tokens, P(group, None), P(group), P("head", None), P(),
    )
    return jax.shard_map(
        shards, mesh=fine, in_specs=placed, out_specs=tokens, check_vma=False
    )
```

```python
import functools

import jax
import jax.numpy as jnp
from jax import lax
from jax.experimental import pallas as pl
from jax.experimental.pallas import tpu as pltpu
from jax.sharding import Mesh, PartitionSpec as P

HS = 128
NZ, NX, NC, NY = 8, 4, 2, 4
GROUPS = 64
ROWS = 256
PART = 64
HEADS = 3
D = 3072
HALF = D // NC
TILE = 768
LAST = 4
SCALE = 1.4426950408889634 * HS**-0.5
NONE = -1e30
MESH_ID = pl.DeviceIdType.MESH
F32, BF16 = jnp.float32, jnp.bfloat16


def kernel(
    hidden_hbm, q_hbm, k_hbm, v_hbm, attends_ref, level_ref, w_hbm, gate_hbm, out_ref,
    qin, vin, kbuf, vbuf, qt, bias_out, bias, acc, top, total, osend, orecv, ssend, srecv,
    att, arecv, wbuf, gates, hidden, summed,
    loc_sem, a2a_send, a2a_recv, bias_send, bias_recv, q_send, q_recv,
    up_send, dn_send, z_recv, sib_send, sib_recv,
    o_send, o_recv, s_send, s_recv, y_loc, y_send, y_recv,
    w_loc, w_send, w_recv, far_send, far_recv, wside_send, wside_recv,
):
    z, x, c, y = (lax.axis_index(a) for a in ("z", "x", "c", "head"))
    above, below = (z + 1) % NZ, (z + NZ - 1) % NZ

    def remote(src, dst, send, recv, dz=None, dx=None, dc=None, dy=None):
        return pltpu.make_async_remote_copy(
            src_ref=src, dst_ref=dst, send_sem=send, recv_sem=recv,
            device_id=(
                z if dz is None else dz, x if dx is None else dx,
                c if dc is None else dc, y if dy is None else dy,
            ),
            device_id_type=MESH_ID,
        )

    def span(at, size):
        return pl.ds(pl.multiple_of(at * size, size), size)

    barrier = pltpu.get_barrier_semaphore()
    peers = [(z, x, c, (y + d) % NY) for d in range(1, NY)]
    peers += [(z, (x + d) % NX, c, y) for d in range(1, NX)]
    peers += [(z, x, 1 - c, y), (above, x, c, y), (below, x, c, y)]
    for peer in peers:
        pl.semaphore_signal(barrier, inc=1, device_id=peer, device_id_type=MESH_ID)

    row = attends_ref[...].astype(F32)
    at_row = lax.broadcasted_iota(jnp.int32, (NZ * NC, GROUPS), 0)
    at_column = lax.broadcasted_iota(jnp.int32, (NZ * NC, GROUPS), 1)
    for place in range(NX):
        group = (at_row // NC) * (NX * NC) + place * NC + at_row % NC
        seen = jnp.sum(jnp.where(at_column == group, row, 0.0), axis=1, keepdims=True)
        bias_out[place] = jnp.broadcast_to(jnp.where(seen > 0.5, 0.0, NONE), (NZ * NC, ROWS))
    bias[x] = bias_out[x]

    pl.semaphore_wait(barrier, len(peers))

    sources = [k_hbm, v_hbm, q_hbm]

    def landing(a, h):
        if a == 0:
            return kbuf.at[z, h, pl.ds(pl.multiple_of(c * ROWS + y * PART, PART), PART), :]
        return (vin if a == 1 else qin).at[h, span(y, PART), :]

    def token_copy(a, h, d):
        dest = (y + d) % NY
        return remote(
            sources[a].at[:, span(dest * HEADS + h, HS)], landing(a, h),
            a2a_send.at[a, h, d - 1], a2a_recv.at[a, h, d - 1], dy=dest,
        )

    def own_copy(a, h):
        return pltpu.make_async_copy(
            sources[a].at[:, span(y * HEADS + h, HS)], landing(a, h), loc_sem.at[a, h]
        )

    for h in range(HEADS):
        for a in range(3):
            for d in (2, 1, 3):
                token_copy(a, h, d).start()
            own_copy(a, h).start()

    def bias_copy(d):
        return remote(
            bias_out.at[(x + d) % NX], bias.at[x], bias_send.at[d - 1], bias_recv.at[d - 1],
            dx=(x + d) % NX,
        )

    for d in range(1, NX):
        bias_copy(d).start()

    def token_wait(a, h):
        own_copy(a, h).wait()
        for d in range(1, NY):
            token_copy(a, h, d).wait_recv()

    def block(kv, b, h, side):
        if kv == 0:
            return kbuf.at[b, h, span(side, ROWS), :]
        return vbuf.at[b, h, :, span(side, ROWS)]

    def up_copy(kv, b, h):
        ref = block(kv, b, h, c)
        return remote(ref, ref, up_send.at[kv, b, h], z_recv.at[kv, b, h], dz=above)

    def down_copy(kv, b, h):
        ref = block(kv, b, h, c)
        return remote(ref, ref, dn_send.at[kv, b, h], z_recv.at[kv, b, h], dz=below)

    def side_copy(kv, b, h, side):
        ref = block(kv, b, h, side)
        return remote(ref, ref, sib_send.at[kv, b, h], sib_recv.at[kv, b, h], dc=1 - c)

    def reaches_up(kv, b, plane):
        near = plane - b <= 3
        if kv == 0:
            near = near | ((plane == NZ - 1) & (b == 3))
        return (plane < NZ) & near

    def reaches_down(kv, b, plane):
        there = (b <= 2) & ((plane >= b + 4) | (plane < b))
        if kv == 1:
            there = there | ((b == 3) & ((plane == NZ - 1) | (plane < b)))
        return there

    def when(condition, act):
        @pl.when(condition)
        def _():
            act()

    def each_move(kv, b, h, moves, act):
        up, down, side = moves
        if up is not None:
            when(up, lambda: act(up_copy(kv, b, h)))
        if down is not None:
            when(down, lambda: act(down_copy(kv, b, h)))
        when(side, lambda: act(side_copy(kv, b, h, c)))

    def start(copy):
        copy.start()

    def own_plan(kv):
        return z < NZ - 1, z <= 2 + kv, z >= 0

    def rising(kv, step):
        b = jnp.maximum(z - step, 0)
        here = (z >= step) & reaches_up(kv, b, z)
        return here, b, (here & reaches_up(kv, b, z + 1), None, here)

    def falling(kv, step):
        b = (z + step) % NZ
        here = reaches_down(kv, b, z)
        return here, b, (None, here & reaches_down(kv, b, below), here & (b < z))

    def query_copy(h, d):
        return remote(
            qt.at[h, x], qt.at[h, x], q_send.at[h, d - 1], q_recv.at[h, d - 1], dx=(x + d) % NX
        )

    for h in range(HEADS):
        token_wait(0, h)
        each_move(0, z, h, own_plan(0), start)
        token_wait(1, h)
        vbuf[z, h, :, span(c, ROWS)] = vin[h].T
        each_move(1, z, h, own_plan(1), start)
        token_wait(2, h)
        qt[h, x] = qin[h].T
        for d in (2, 1, 3):
            query_copy(h, d).start()

    def weight_rows(owner, part):
        if part is None:
            return span(owner, HS)
        return pl.ds(pl.multiple_of(owner * HS + part * (HS // 2), HS // 2), HS // 2)

    def weight_ref(h, owner, part, half):
        return wbuf.at[h, weight_rows(owner, part), span(half, HALF)]

    ahead, behind, opposite = (y + 1) % NY, (y + NY - 1) % NY, (y + 2) % NY

    def weight_copy(h, way):
        return remote(
            w_hbm.at[h, :, span(c, HALF)], weight_ref(h, y, None, c),
            w_send.at[h, way], w_recv.at[h, way], dy=(ahead, behind)[way],
        )

    def far_copy(h, way):
        ref = weight_ref(h, (behind, ahead)[way], way, c)
        return remote(
            ref, ref, far_send.at[h, way], far_recv.at[h, way], dy=(ahead, behind)[way]
        )

    def weight_side(h, piece):
        owner, part = ((behind, None), (ahead, None), (opposite, 0), (opposite, 1))[piece]
        ref = weight_ref(h, owner, part, c)
        return remote(ref, ref, wside_send.at[h, piece], wside_recv.at[h, piece], dc=1 - c)

    own_weight = pltpu.make_async_copy(w_hbm, wbuf.at[:, weight_rows(y, None), :], w_loc.at[0])
    gate_copy = pltpu.make_async_copy(gate_hbm, gates, w_loc.at[1])
    hidden_copy = pltpu.make_async_copy(hidden_hbm, hidden, w_loc.at[2])
    for h in range(HEADS):
        for way in range(2):
            weight_copy(h, way).start()
    own_weight.start()
    gate_copy.start()
    hidden_copy.start()

    def weight_near(h):
        for way in range(2):
            weight_copy(h, way).wait_recv()
            far_copy(h, way).start()
            weight_side(h, way).start()

    acc[...] = jnp.zeros_like(acc)
    top[...] = jnp.full_like(top, NONE)
    total[...] = jnp.zeros_like(total)

    def query_wait(h, d):
        ref = qt.at[h, (x + NX - d) % NX]
        remote(ref, ref, q_send.at[h, d - 1], q_recv.at[h, d - 1], dx=(x + d) % NX).wait_recv()

    def bias_wait(d):
        ref = bias.at[(x + NX - d) % NX]
        remote(ref, ref, bias_send.at[d - 1], bias_recv.at[d - 1], dx=(x + d) % NX).wait_recv()

    def attend(blocks, h):
        scores = [
            [jnp.dot(kbuf[b, h], qt[h, r], preferred_element_type=F32) for b in blocks]
            for r in range(NX)
        ]
        for r in range(NX):
            parts, offs = [], []
            for i, b in enumerate(blocks):
                for s in range(NC):
                    parts.append(scores[r][i][s * ROWS : (s + 1) * ROWS])
                    offs.append(bias[r, pl.ds(b * NC + s, 1), :])
            old = top[h, r]
            new = old
            for p, o in zip(parts, offs):
                new = jnp.maximum(new, jnp.max(p, axis=0, keepdims=True) + o)
            factor = jnp.exp2((old - new) * SCALE)
            weights = [jnp.exp2(p * SCALE + (o - new * SCALE)) for p, o in zip(parts, offs)]
            top[h, r] = new
            total[h, r] = total[h, r] * factor + sum(
                jnp.sum(w, axis=0, keepdims=True) for w in weights
            )
            rounded = [w.astype(BF16) for w in weights]
            added = sum(
                jnp.dot(
                    vbuf[b, h], jnp.concatenate(rounded[NC * i : NC * i + NC], axis=0),
                    preferred_element_type=F32,
                )
                for i, b in enumerate(blocks)
            )
            acc[h, r] = acc[h, r] * factor + added

    def arrive(step, h):
        for kv in range(2):
            for plan in (rising, falling):
                here, b, moves = plan(kv, step)

                def take(kv=kv, b=b, moves=moves):
                    up_copy(kv, b, h).wait_recv()
                    each_move(kv, b, h, moves, start)

                when(here, take)

    def side_wait(b, h):
        for kv in range(2):
            side_copy(kv, b, h, 1 - c).wait_recv()

    def result_copy(h, d):
        return remote(
            osend.at[h, d - 1], orecv.at[h, d - 1], o_send.at[h, d - 1], o_recv.at[h, d - 1],
            dx=(x + d) % NX,
        )

    def stats_copy(h, d):
        return remote(
            ssend.at[h, d - 1], srecv.at[h, d - 1], s_send.at[h, d - 1], s_recv.at[h, d - 1],
            dx=(x + d) % NX,
        )

    def hand_over(h):
        for d in (2, 1, 3):
            r = (x + d) % NX
            ssend[h, d - 1, 0:1] = top[h, r]
            ssend[h, d - 1, 1:2] = total[h, r]
            stats_copy(h, d).start()
            osend[h, d - 1] = acc[h, r].astype(BF16)
            result_copy(h, d).start()

    @pl.loop(0, (LAST + 1) * HEADS)
    def _(i):
        step, h = i // HEADS, i % HEADS

        @pl.when(step < LAST - 1)
        def _():
            arrive(step + 1, h)

        @pl.when(step == LAST)
        def _():
            arrive(step, h)

        @pl.when(step == 0)
        def _():
            for d in range(1, NX):
                query_wait(h, d)

        @pl.when(i == 0)
        def _():
            for d in range(1, NX):
                bias_wait(d)

        low = jnp.maximum(z - step, 0)
        high = (z + step) % NZ
        has_low = (z >= step) & reaches_up(0, low, z)
        has_high = (step > 0) & reaches_down(0, high, z) & (high < z)
        when(has_low, lambda: side_wait(low, h))
        when(has_high, lambda: side_wait(high, h))
        when(has_low & has_high, lambda: attend([low, high], h))
        when(
            has_low != has_high,
            lambda: attend([jnp.where(has_low, low, high)], h),
        )

        for at, piece in ((4, 0), (7, 1), (11, 2)):
            when(i == at, lambda piece=piece: weight_near(piece))

        when(step == LAST, lambda: hand_over(h))

    def back_copy(h, d):
        dest = (y + d) % NY
        return remote(
            att.at[h, span(dest, PART), :], arecv.at[h, :, span(y, HS)],
            y_send.at[h, d - 1], y_recv.at[h, d - 1], dy=dest,
        )

    def keep_copy(h):
        return pltpu.make_async_copy(
            att.at[h, span(y, PART), :], arecv.at[h, :, span(y, HS)], y_loc.at[h]
        )

    for h in range(HEADS):
        for d in range(1, NX):
            stats_copy(h, d).wait_recv()
            result_copy(h, d).wait_recv()
        tops = [top[h, x]] + [srecv[h, d, 0:1] for d in range(NX - 1)]
        totals = [total[h, x]] + [srecv[h, d, 1:2] for d in range(NX - 1)]
        best = functools.reduce(jnp.maximum, tops)
        shares = [jnp.exp2((t - best) * SCALE) for t in tops]
        inverse = 1.0 / sum(s * t for s, t in zip(shares, totals))
        parts = [acc[h, x]] + [orecv[h, d].astype(F32) for d in range(NX - 1)]
        merged = sum(p * (s * inverse) for p, s in zip(parts, shares))
        att[h] = merged.astype(BF16).T
        for d in (2, 1, 3):
            back_copy(h, d).start()
        keep_copy(h).start()

    gate_copy.wait()
    hidden_copy.wait()
    own_weight.wait()
    for h in range(HEADS):
        for way in range(2):
            far_copy(h, way).wait_recv()
            weight_side(h, 2 + way).start()
        for piece in range(2):
            weight_side(h, piece).wait_recv()
        keep_copy(h).wait()
        for d in range(1, NY):
            back_copy(h, d).wait_recv()
        for piece in range(2, 4):
            weight_side(h, piece).wait_recv()

        @pl.loop(0, D // TILE)
        def _(j, h=h):
            columns = span(j, TILE)
            part = jnp.dot(arecv[h], wbuf[h, :, columns], preferred_element_type=F32)
            if h > 0:
                part = part + summed[:, columns]
            if h < HEADS - 1:
                summed[:, columns] = part
            else:
                gated = gates[pl.ds(level_ref[0], 1), columns] * part
                out_ref[:, columns] = (hidden[:, columns].astype(F32) + gated).astype(BF16)

    def ended(copy):
        copy.wait_send()

    for h in range(HEADS):
        for d in range(1, NY):
            for a in range(3):
                token_copy(a, h, d).wait_send()
            query_copy(h, d).wait_send()
            result_copy(h, d).wait_send()
            stats_copy(h, d).wait_send()
            back_copy(h, d).wait_send()
        for way in range(2):
            weight_copy(h, way).wait_send()
            far_copy(h, way).wait_send()
        for piece in range(4):
            weight_side(h, piece).wait_send()
        for kv in range(2):
            each_move(kv, z, h, own_plan(kv), ended)
    for d in range(1, NX):
        bias_copy(d).wait_send()

    @pl.loop(HEADS, (LAST + 1) * HEADS)
    def _(i):
        step, h = i // HEADS, i % HEADS
        for kv in range(2):
            for plan in (rising, falling):
                _, b, moves = plan(kv, step)
                each_move(kv, b, h, moves, ended)


def fused(hidden, query, keys, values, attends, levels, weight, gate_table):
    dma = pltpu.SemaphoreType.DMA
    vmem = pltpu.VMEM
    hbm = pl.BlockSpec(memory_space=pltpu.HBM)
    local = pl.BlockSpec(memory_space=pltpu.VMEM)
    others = (HEADS, NX - 1)
    moving = (2, NZ, HEADS)
    return pl.pallas_call(
        kernel,
        out_shape=jax.ShapeDtypeStruct((PART, D), BF16),
        in_specs=[
            hbm, hbm, hbm, hbm, local, pl.BlockSpec(memory_space=pltpu.SMEM), hbm, hbm,
        ],
        out_specs=local,
        scratch_shapes=[
            vmem((HEADS, ROWS, HS), BF16),
            vmem((HEADS, ROWS, HS), BF16),
            vmem((NZ, HEADS, NC * ROWS, HS), BF16),
            vmem((NZ, HEADS, HS, NC * ROWS), BF16),
            vmem((HEADS, NX, HS, ROWS), BF16),
            vmem((NX, NZ * NC, ROWS), F32),
            vmem((NX, NZ * NC, ROWS), F32),
            vmem((HEADS, NX, HS, ROWS), F32),
            vmem((HEADS, NX, 1, ROWS), F32),
            vmem((HEADS, NX, 1, ROWS), F32),
            vmem((HEADS, NX - 1, HS, ROWS), BF16),
            vmem((HEADS, NX - 1, HS, ROWS), BF16),
            vmem((HEADS, NX - 1, 2, ROWS), F32),
            vmem((HEADS, NX - 1, 2, ROWS), F32),
            vmem((HEADS, ROWS, HS), BF16),
            vmem((HEADS, PART, NY * HS), BF16),
            vmem((HEADS, NY * HS, D), BF16),
            vmem((GROUPS, D), F32),
            vmem((PART, D), BF16),
            vmem((PART, D), F32),
            dma((3, HEADS)), dma((3, HEADS, NY - 1)), dma((3, HEADS, NY - 1)),
            dma((NX - 1,)), dma((NX - 1,)), dma(others), dma(others),
            dma(moving), dma(moving), dma(moving), dma(moving), dma(moving),
            dma(others), dma(others), dma(others), dma(others),
            dma((HEADS,)), dma(others), dma(others),
            dma((3,)), dma((HEADS, 2)), dma((HEADS, 2)), dma((HEADS, 2)), dma((HEADS, 2)),
            dma((HEADS, 4)), dma((HEADS, 4)),
        ],
        compiler_params=pltpu.CompilerParams(
            collective_id=0, has_side_effects=True, vmem_limit_bytes=48 * 1024 * 1024
        ),
    )(hidden, query, keys, values, attends, levels, weight, gate_table)


def shards(hidden, query, keys, values, attends, levels, out_weight, gate_table):
    weight = out_weight.reshape(HEADS, HS, D)
    return fused(hidden, query, keys, values, attends, levels, weight, gate_table)


def solution(mesh):
    fine = Mesh(mesh.devices.reshape(NZ, NX, NC, NY), ("z", "x", "c", "head"))
    tokens = P(("z", "x", "c", "head"), None)
    group = ("z", "x", "c")
    placed = (
        tokens, tokens, tokens, tokens, P(group, None), P(group), P("head", None), P(),
    )
    return jax.shard_map(
        shards, mesh=fine, in_specs=placed, out_specs=tokens, check_vma=False
    )
```

```python
import functools

import jax
import jax.numpy as jnp
from jax import lax
from jax.experimental import pallas as pl
from jax.experimental.pallas import tpu as pltpu
from jax.sharding import Mesh, PartitionSpec as P

HS = 128
NZ, NX, NC, NY = 8, 4, 2, 4
GROUPS = 64
ROWS = 256
PART = 64
HEADS = 3
D = 3072
HALF = D // NC
TILE = 768
LAST = 4
SCALE = 1.4426950408889634 * HS**-0.5
NONE = -1e30
MESH_ID = pl.DeviceIdType.MESH
F32, BF16 = jnp.float32, jnp.bfloat16


def kernel(
    hidden_hbm, q_hbm, k_hbm, v_hbm, attends_hbm, level_ref, w_hbm, gate_hbm, out_hbm,
    attends, qin, kvin, kv, qt, bias_out, bias, acc, top, total, osend, orecv, ssend, srecv,
    att, arecv, wbuf, gates, hidden, summed, out,
    early_sem, token_send, kv_sem, q_sem, bias_send, bias_recv, q_send, q_recv,
    up_send, dn_send, z_recv, sib_send, sib_recv,
    o_send, o_recv, s_send, s_recv, y_send, y_recv,
    w_send, w_recv, far_send, far_recv, near_send, near_recv, side_send, side_recv, out_sem,
):
    z, x, c, y = (lax.axis_index(a) for a in ("z", "x", "c", "head"))
    above, below = (z + 1) % NZ, (z + NZ - 1) % NZ

    def remote(src, dst, send, recv, dz=None, dx=None, dc=None, dy=None):
        return pltpu.make_async_remote_copy(
            src_ref=src, dst_ref=dst, send_sem=send, recv_sem=recv,
            device_id=(
                z if dz is None else dz, x if dx is None else dx,
                c if dc is None else dc, y if dy is None else dy,
            ),
            device_id_type=MESH_ID,
        )

    def span(at, size):
        return pl.ds(pl.multiple_of(at * size, size), size)

    def wait_bytes(ref, sem):
        pltpu.make_async_copy(ref, ref, sem).wait()

    attends_copy = pltpu.make_async_copy(attends_hbm, attends, early_sem.at[0])
    own_weight = pltpu.make_async_copy(w_hbm, wbuf.at[:, span(y, HS), :], early_sem.at[1])
    gate_copy = pltpu.make_async_copy(gate_hbm, gates, early_sem.at[2])
    hidden_copy = pltpu.make_async_copy(hidden_hbm, hidden, early_sem.at[3])
    attends_copy.start()

    barrier = pltpu.get_barrier_semaphore()
    peers = [(z, x, c, (y + d) % NY) for d in range(1, NY)]
    peers += [(z, (x + d) % NX, c, y) for d in range(1, NX)]
    peers += [(z, x, 1 - c, y), (above, x, c, y), (below, x, c, y)]
    for peer in peers:
        pl.semaphore_signal(barrier, inc=1, device_id=peer, device_id_type=MESH_ID)
    pl.semaphore_wait(barrier, len(peers))

    sources = [k_hbm, v_hbm, q_hbm]

    def landing(a, h):
        return (kvin.at[h, a] if a < 2 else qin.at[h]).at[span(y, PART), :]

    def landed(a, h):
        return (kv_sem if a < 2 else q_sem).at[h]

    def token_copy(a, h, d):
        dest = (y + d) % NY
        return remote(
            sources[a].at[:, span(dest * HEADS + h, HS)], landing(a, h),
            token_send.at[a], landed(a, h), dy=dest,
        )

    for h in range(HEADS):
        for a in range(3):
            for d in (2, 1, 3):
                token_copy(a, h, d).start()
            pltpu.make_async_copy(
                sources[a].at[:, span(y * HEADS + h, HS)], landing(a, h), landed(a, h)
            ).start()

    def up_copy(b, h):
        ref = kv.at[b, h, c]
        return remote(ref, ref, up_send.at[b, h], z_recv.at[b, h], dz=above)

    def down_copy(b, h):
        ref = kv.at[b, h, c]
        return remote(ref, ref, dn_send.at[b, h], z_recv.at[b, h], dz=below)

    def side_copy(b, h, side):
        ref = kv.at[b, h, side]
        return remote(ref, ref, sib_send.at[b, h], sib_recv.at[b, h], dc=1 - c)

    def reaches_up(b, h, plane):
        return (plane < NZ) & ((plane - b <= 3) | ((plane == NZ - 1) & (b == 3) & (h < 2)))

    def reaches_down(b, h, plane):
        return ((b <= 2) & ((plane >= b + 4) | (plane < b))) | (
            (b == 3) & (h == 2) & ((plane == NZ - 1) | (plane < b))
        )

    def when(condition, act):
        @pl.when(condition)
        def _():
            act()

    def each_move(b, h, moves, act):
        up, down, side = moves
        if up is not None:
            when(up, lambda: act(up_copy(b, h)))
        if down is not None:
            when(down, lambda: act(down_copy(b, h)))
        when(side, lambda: act(side_copy(b, h, c)))

    def start(copy):
        copy.start()

    def ended(copy):
        copy.wait_send()

    def own_plan(h):
        return z < NZ - 1, z <= (3 if h == 2 else 2), z >= 0

    def rising(step, h):
        b = jnp.maximum(z - step, 0)
        here = (z >= step) & reaches_up(b, h, z)
        return here, b, (here & reaches_up(b, h, z + 1), None, here)

    def falling(step, h):
        b = (z + step) % NZ
        here = reaches_down(b, h, z)
        return here, b, (None, here & reaches_down(b, h, below), here & (b < z))

    def query_copy(h, d):
        return remote(qt.at[h, x], qt.at[h, x], q_send.at[h], q_recv.at[h], dx=(x + d) % NX)

    ahead, behind, opposite = (y + 1) % NY, (y + NY - 1) % NY, (y + 2) % NY

    def weight_ref(h, owner, part):
        rows = span(owner, HS) if part is None else span(owner * 2 + part, HS // 2)
        return wbuf.at[h, rows, span(c, HALF)]

    def weight_bytes(h, rows):
        return wbuf.at[h, 0:rows, 0:HALF]

    def weight_copy(h, way):
        return remote(
            w_hbm.at[h, :, span(c, HALF)], weight_ref(h, y, None),
            w_send.at[h], w_recv.at[h], dy=(ahead, behind)[way],
        )

    def far_copy(h, way):
        ref = weight_ref(h, (behind, ahead)[way], way)
        return remote(ref, ref, far_send.at[h], far_recv.at[h], dy=(ahead, behind)[way])

    def near_side(h, way):
        ref = weight_ref(h, (behind, ahead)[way], None)
        return remote(ref, ref, near_send.at[h], near_recv.at[h], dc=1 - c)

    def far_side(h, way):
        ref = weight_ref(h, opposite, way)
        return remote(ref, ref, side_send.at[h], side_recv.at[h], dc=1 - c)

    def weight_start(h):
        for way in range(2):
            weight_copy(h, way).start()

    def weight_near(h):
        wait_bytes(weight_bytes(h, 2 * HS), w_recv.at[h])
        for way in range(2):
            far_copy(h, way).start()
        for way in range(2):
            near_side(h, way).start()

    def weight_far(h):
        wait_bytes(weight_bytes(h, HS), far_recv.at[h])
        for way in range(2):
            far_side(h, way).start()

    for h in range(HEADS):
        wait_bytes(kvin.at[h], kv_sem.at[h])
        kv[z, h, c, 0:ROWS, :] = kvin[h, 0]
        turned = kvin[h, 1].T
        kv[z, h, c, ROWS : ROWS + HS, :] = turned[:, :HS]
        kv[z, h, c, ROWS + HS :, :] = turned[:, HS:]
        each_move(z, h, own_plan(h), start)
        wait_bytes(qin.at[h], q_sem.at[h])
        qt[h, x] = qin[h].T
        for d in (2, 1, 3):
            query_copy(h, d).start()
        weight_start(h)

    attends_copy.wait()
    row = attends[...].astype(F32)
    at_row = lax.broadcasted_iota(jnp.int32, (NZ * NC, GROUPS), 0)
    at_column = lax.broadcasted_iota(jnp.int32, (NZ * NC, GROUPS), 1)
    for place in range(NX):
        group = (at_row // NC) * (NX * NC) + place * NC + at_row % NC
        seen = jnp.sum(jnp.where(at_column == group, row, 0.0), axis=1, keepdims=True)
        bias_out[place] = jnp.broadcast_to(jnp.where(seen > 0.5, 0.0, NONE), (NZ * NC, ROWS))
    bias[x] = bias_out[x]

    def bias_copy(d):
        return remote(bias_out.at[(x + d) % NX], bias.at[x], bias_send, bias_recv, dx=(x + d) % NX)

    for d in range(1, NX):
        bias_copy(d).start()
    own_weight.start()
    gate_copy.start()
    hidden_copy.start()
    acc[...] = jnp.zeros_like(acc)
    top[...] = jnp.full_like(top, NONE)
    total[...] = jnp.zeros_like(total)

    def attend(blocks, h):
        keys = [jnp.concatenate([kv[b, h, s, :ROWS] for s in range(NC)], axis=0) for b in blocks]
        values = [
            jnp.concatenate(
                [kv[b, h, s, ROWS + i * HS : ROWS + i * HS + HS] for s in range(NC) for i in (0, 1)],
                axis=1,
            )
            for b in blocks
        ]
        scores = [
            [jnp.dot(k, qt[h, r], preferred_element_type=F32) for k in keys] for r in range(NX)
        ]
        for r in range(NX):
            parts, offs = [], []
            for i, b in enumerate(blocks):
                for s in range(NC):
                    parts.append(scores[r][i][s * ROWS : (s + 1) * ROWS])
                    offs.append(bias[r, pl.ds(b * NC + s, 1), :])
            old = top[h, r]
            new = old
            for p, o in zip(parts, offs):
                new = jnp.maximum(new, jnp.max(p, axis=0, keepdims=True) + o)
            factor = jnp.exp2((old - new) * SCALE)
            weights = [jnp.exp2(p * SCALE + (o - new * SCALE)) for p, o in zip(parts, offs)]
            top[h, r] = new
            total[h, r] = total[h, r] * factor + sum(
                jnp.sum(w, axis=0, keepdims=True) for w in weights
            )
            rounded = [w.astype(BF16) for w in weights]
            added = sum(
                jnp.dot(
                    v, jnp.concatenate(rounded[NC * i : NC * i + NC], axis=0),
                    preferred_element_type=F32,
                )
                for i, v in enumerate(values)
            )
            acc[h, r] = acc[h, r] * factor + added

    def arrive(step, h):
        for plan in (rising, falling):
            here, b, moves = plan(step, h)

            def take(b=b, moves=moves):
                up_copy(b, h).wait_recv()
                each_move(b, h, moves, start)

            when(here, take)

    def result_copy(h, d):
        return remote(
            osend.at[h, d - 1], orecv.at[h, d - 1], o_send.at[h], o_recv.at[h], dx=(x + d) % NX
        )

    def stats_copy(h, d):
        return remote(
            ssend.at[h, d - 1], srecv.at[h, d - 1], s_send.at[h], s_recv.at[h], dx=(x + d) % NX
        )

    def hand_over(h):
        for d in (2, 1, 3):
            r = (x + d) % NX
            ssend[h, d - 1, 0:1] = top[h, r]
            ssend[h, d - 1, 1:2] = total[h, r]
            stats_copy(h, d).start()
            osend[h, d - 1] = acc[h, r].astype(BF16)
            result_copy(h, d).start()

    def back_copy(h, d):
        dest = (y + d) % NY
        return remote(
            att.at[h, span(dest, PART), :], arecv.at[h, :, span(y, HS)],
            y_send.at[h], y_recv.at[h], dy=dest,
        )

    def merge(h):
        wait_bytes(srecv.at[h], s_recv.at[h])
        wait_bytes(orecv.at[h], o_recv.at[h])
        tops = [top[h, x]] + [srecv[h, d, 0:1] for d in range(NX - 1)]
        totals = [total[h, x]] + [srecv[h, d, 1:2] for d in range(NX - 1)]
        best = functools.reduce(jnp.maximum, tops)
        shares = [jnp.exp2((t - best) * SCALE) for t in tops]
        inverse = 1.0 / sum(s * t for s, t in zip(shares, totals))
        parts = [acc[h, x]] + [orecv[h, d].astype(F32) for d in range(NX - 1)]
        merged = sum(p * (s * inverse) for p, s in zip(parts, shares))
        att[h] = merged.astype(BF16).T
        for d in (2, 1, 3):
            back_copy(h, d).start()
        pltpu.make_async_copy(
            att.at[h, span(y, PART), :], arecv.at[h, :, span(y, HS)], y_recv.at[h]
        ).start()

    def settle(h):
        wait_bytes(qt.at[h, 0 : NX - 1], q_send.at[h])
        each_move(z, h, (z < NZ - 1, (z <= 2) | ((z == 3) & (h == 2)), z >= 0), ended)

        @pl.loop(1, LAST + 1)
        def _(step):
            for plan in (rising, falling):
                _, b, moves = plan(step, h)
                each_move(b, h, moves, ended)

    @pl.loop(0, (LAST + 1) * HEADS + 1)
    def _(i):
        step, h = i // HEADS, i % HEADS

        when(step < LAST - 1, lambda: arrive(step + 1, h))
        when(step == LAST, lambda: arrive(step, h))
        when(step == 0, lambda: wait_bytes(qt.at[h, 0 : NX - 1], q_recv.at[h]))
        when(i == 0, lambda: wait_bytes(bias.at[0 : NX - 1], bias_recv))

        low = jnp.maximum(z - step, 0)
        high = (z + step) % NZ
        has_low = (step <= LAST) & (z >= step) & reaches_up(low, h, z)
        has_high = (step > 0) & (step <= LAST) & reaches_down(high, h, z) & (high < z)
        when(has_low, lambda: side_copy(low, h, 1 - c).wait_recv())
        when(has_high, lambda: side_copy(high, h, 1 - c).wait_recv())
        when(has_low & has_high, lambda: attend([low, high], h))
        when(has_low != has_high, lambda: attend([jnp.where(has_low, low, high)], h))

        for at, piece in ((4, 0), (7, 1), (11, 2)):
            when(i == at, lambda piece=piece: weight_near(piece))

        @pl.when(step == LAST)
        def _():
            hand_over(h)
            settle(h)

        when(i > LAST * HEADS, lambda: merge((i - 1) % HEADS))

    weight_far(0)
    for a in range(3):
        wait_bytes(sources[a].at[:, 0 : 3 * HEADS * HS], token_send.at[a])
    wait_bytes(bias.at[0 : NX - 1], bias_send)
    gate_copy.wait()
    hidden_copy.wait()
    own_weight.wait()

    def out_copy(j):
        columns = pl.ds(j * TILE, TILE)
        return pltpu.make_async_copy(out.at[:, columns], out_hbm.at[:, columns], out_sem.at[j])

    for h in range(HEADS):
        if h > 0:
            weight_far(h)
        wait_bytes(weight_bytes(h, 2 * HS), near_recv.at[h])
        wait_bytes(arecv.at[h], y_recv.at[h])
        wait_bytes(weight_bytes(h, HS), side_recv.at[h])
        for j in range(D // TILE):
            columns = slice(j * TILE, (j + 1) * TILE)
            part = jnp.dot(arecv[h], wbuf[h, :, columns], preferred_element_type=F32)
            if h > 0:
                part = part + summed[:, columns]
            if h < HEADS - 1:
                summed[:, columns] = part
            else:
                gated = gates[pl.ds(level_ref[0], 1), columns] * part
                out[:, columns] = (hidden[:, columns].astype(F32) + gated).astype(BF16)
                out_copy(j).start()

    for h in range(HEADS):
        wait_bytes(osend.at[h], o_send.at[h])
        wait_bytes(ssend.at[h], s_send.at[h])
        wait_bytes(att.at[h, 0 : 3 * PART], y_send.at[h])
        wait_bytes(weight_bytes(h, 2 * HS), w_send.at[h])
        wait_bytes(weight_bytes(h, HS), far_send.at[h])
        wait_bytes(weight_bytes(h, 2 * HS), near_send.at[h])
        wait_bytes(weight_bytes(h, HS), side_send.at[h])
    for j in range(D // TILE):
        out_copy(j).wait()


def fused(hidden, query, keys, values, attends, levels, weight, gate_table):
    dma = pltpu.SemaphoreType.DMA
    vmem = pltpu.VMEM
    hbm = pl.BlockSpec(memory_space=pltpu.HBM)
    each = dma((HEADS,))
    moving = dma((NZ, HEADS))
    return pl.pallas_call(
        kernel,
        out_shape=jax.ShapeDtypeStruct((PART, D), BF16),
        in_specs=[hbm, hbm, hbm, hbm, hbm, pl.BlockSpec(memory_space=pltpu.SMEM), hbm, hbm],
        out_specs=hbm,
        scratch_shapes=[
            vmem((1, GROUPS), jnp.int32),
            vmem((HEADS, ROWS, HS), BF16),
            vmem((HEADS, 2, ROWS, HS), BF16),
            vmem((NZ, HEADS, NC, 2 * ROWS, HS), BF16),
            vmem((HEADS, NX, HS, ROWS), BF16),
            vmem((NX, NZ * NC, ROWS), F32),
            vmem((NX, NZ * NC, ROWS), F32),
            vmem((HEADS, NX, HS, ROWS), F32),
            vmem((HEADS, NX, 1, ROWS), F32),
            vmem((HEADS, NX, 1, ROWS), F32),
            vmem((HEADS, NX - 1, HS, ROWS), BF16),
            vmem((HEADS, NX - 1, HS, ROWS), BF16),
            vmem((HEADS, NX - 1, 2, ROWS), F32),
            vmem((HEADS, NX - 1, 2, ROWS), F32),
            vmem((HEADS, ROWS, HS), BF16),
            vmem((HEADS, PART, NY * HS), BF16),
            vmem((HEADS, NY * HS, D), BF16),
            vmem((GROUPS, D), F32),
            vmem((PART, D), BF16),
            vmem((PART, D), F32),
            vmem((PART, D), BF16),
            dma((4,)), dma((3,)), each, each, dma(()), dma(()), each, each,
            moving, moving, moving, moving, moving,
            each, each, each, each, each, each,
            each, each, each, each, each, each, each, each, dma((D // TILE,)),
        ],
        compiler_params=pltpu.CompilerParams(
            collective_id=0, has_side_effects=True, vmem_limit_bytes=60 * 1024 * 1024
        ),
    )(hidden, query, keys, values, attends, levels, weight, gate_table)


def shards(hidden, query, keys, values, attends, levels, out_weight, gate_table):
    weight = out_weight.reshape(HEADS, HS, D)
    return fused(hidden, query, keys, values, attends, levels, weight, gate_table)


def solution(mesh):
    fine = Mesh(mesh.devices.reshape(NZ, NX, NC, NY), ("z", "x", "c", "head"))
    tokens = P(("z", "x", "c", "head"), None)
    group = ("z", "x", "c")
    placed = (
        tokens, tokens, tokens, tokens, P(group, None), P(group), P("head", None), P(),
    )
    return jax.shard_map(
        shards, mesh=fine, in_specs=placed, out_specs=tokens, check_vma=False
    )
```

```python
import functools

import jax
import jax.numpy as jnp
from jax import lax
from jax.experimental import pallas as pl
from jax.experimental.pallas import tpu as pltpu
from jax.sharding import Mesh, PartitionSpec as P

HS = 128
NZ, NX, NC, NY = 8, 4, 2, 4
GROUPS = 64
ROWS = 256
PART = 64
HEADS = 3
D = 3072
HALF = D // NC
TILE = 768
LAST = 4
SCALE = 1.4426950408889634 * HS**-0.5
NONE = -1e30
ORDER = tuple((s, h) for s in range(3) for h in range(3)) + (
    (3, 0), (3, 1), (4, 0), (3, 2), (4, 2), (4, 1),
)
TAKEN = (3, 4, 5, 5, 6, 7, 8, 8, 9, 10, 11, 12, 13, 14, 14)
MESH_ID = pl.DeviceIdType.MESH
F32, BF16 = jnp.float32, jnp.bfloat16


def kernel(
    hidden_hbm, q_hbm, k_hbm, v_hbm, attends_hbm, level_ref, w_hbm, gate_hbm, out_hbm,
    attends, qin, kvin, kv, qt, bias_out, bias, acc, top, total, osend, orecv, ssend, srecv,
    att, arecv, wbuf, gates, hidden, summed, out,
    early_sem, token_send, kv_sem, q_sem, bias_send, bias_recv, q_send, q_recv,
    up_send, dn_send, z_recv, sib_send, sib_recv,
    o_send, o_recv, s_send, s_recv, y_send, y_recv,
    w_send, w_recv, far_send, far_recv, swap_send, swap_recv, swap_far_send, swap_far_recv,
    near_send, near_recv, side_send, side_recv, out_sem,
):
    z, x, c, y = (lax.axis_index(a) for a in ("z", "x", "c", "head"))
    above, below = (z + 1) % NZ, (z + NZ - 1) % NZ

    def remote(src, dst, send, recv, dz=None, dx=None, dc=None, dy=None):
        return pltpu.make_async_remote_copy(
            src_ref=src, dst_ref=dst, send_sem=send, recv_sem=recv,
            device_id=(
                z if dz is None else dz, x if dx is None else dx,
                c if dc is None else dc, y if dy is None else dy,
            ),
            device_id_type=MESH_ID,
        )

    def span(at, size):
        return pl.ds(pl.multiple_of(at * size, size), size)

    def wait_bytes(ref, sem):
        pltpu.make_async_copy(ref, ref, sem).wait()

    attends_copy = pltpu.make_async_copy(attends_hbm, attends, early_sem.at[0])
    own_weight = pltpu.make_async_copy(w_hbm, wbuf.at[:, span(y, HS), :], early_sem.at[1])
    gate_copy = pltpu.make_async_copy(gate_hbm, gates, early_sem.at[2])
    hidden_copy = pltpu.make_async_copy(hidden_hbm, hidden, early_sem.at[3])
    attends_copy.start()

    barrier = pltpu.get_barrier_semaphore()
    peers = [(z, x, c, (y + d) % NY) for d in range(1, NY)]
    peers += [(z, (x + d) % NX, c, y) for d in range(1, NX)]
    peers += [(z, x, 1 - c, y), (above, x, c, y), (below, x, c, y)]
    for peer in peers:
        pl.semaphore_signal(barrier, inc=1, device_id=peer, device_id_type=MESH_ID)
    pl.semaphore_wait(barrier, len(peers))

    sources = [k_hbm, v_hbm, q_hbm]

    def landing(a, h):
        return (kvin.at[h, a] if a < 2 else qin.at[h]).at[span(y, PART), :]

    def landed(a, h):
        return (kv_sem if a < 2 else q_sem).at[h]

    def token_copy(a, h, d):
        dest = (y + d) % NY
        return remote(
            sources[a].at[:, span(dest * HEADS + h, HS)], landing(a, h),
            token_send.at[a], landed(a, h), dy=dest,
        )

    def token_start(h):
        for a in range(3):
            for d in (2, 1, 3):
                token_copy(a, h, d).start()
            pltpu.make_async_copy(
                sources[a].at[:, span(y * HEADS + h, HS)], landing(a, h), landed(a, h)
            ).start()

    token_start(0)
    token_start(1)

    def up_copy(b, h):
        ref = kv.at[b, h, c]
        return remote(ref, ref, up_send.at[b, h], z_recv.at[b, h], dz=above)

    def down_copy(b, h):
        ref = kv.at[b, h, c]
        return remote(ref, ref, dn_send.at[b, h], z_recv.at[b, h], dz=below)

    def side_copy(b, h, side):
        ref = kv.at[b, h, side]
        return remote(ref, ref, sib_send.at[b, h], sib_recv.at[b, h], dc=1 - c)

    def reaches_up(b, h, plane):
        return (plane < NZ) & ((plane - b <= 3) | ((plane == NZ - 1) & (b == 3) & (h < 2)))

    def reaches_down(b, h, plane):
        return ((b <= 2) & ((plane >= b + 4) | (plane < b))) | (
            (b == 3) & (h == 2) & ((plane == NZ - 1) | (plane < b))
        )

    def when(condition, act):
        @pl.when(condition)
        def _():
            act()

    def each_move(b, h, moves, act):
        up, down, side = moves
        if up is not None:
            when(up, lambda: act(up_copy(b, h)))
        if down is not None:
            when(down, lambda: act(down_copy(b, h)))
        when(side, lambda: act(side_copy(b, h, c)))

    def start(copy):
        copy.start()

    def ended(copy):
        copy.wait_send()

    def own_plan(h):
        return z < NZ - 1, z <= (3 if h == 2 else 2), z >= 0

    def rising(step, h):
        b = jnp.maximum(z - step, 0)
        here = (z >= step) & reaches_up(b, h, z)
        return here, b, (here & reaches_up(b, h, z + 1), None, here)

    def falling(step, h):
        b = (z + step) % NZ
        here = reaches_down(b, h, z)
        return here, b, (None, here & reaches_down(b, h, below), here & (b < z))

    def query_copy(h, d):
        return remote(qt.at[h, x], qt.at[h, x], q_send.at[h], q_recv.at[h], dx=(x + d) % NX)

    ahead, behind, opposite = (y + 1) % NY, (y + NY - 1) % NY, (y + 2) % NY

    odd = x % 2
    partner = ((x + 1 - 2 * odd) % NX, (x + NX - 1 + 2 * odd) % NX)

    def weight_ref(h, owner, part, parts):
        size = HS // parts
        rows = pl.ds(pl.multiple_of(owner * HS + part * size, size), size)
        return wbuf.at[h, rows, span(c, HALF)]

    def weight_bytes(h, rows):
        return wbuf.at[h, 0:rows, 0:HALF]

    def shared(h):
        return h < 1

    def fetched(h, owner):
        return weight_ref(h, owner, odd, 2) if shared(h) else weight_ref(h, owner, 0, 1)

    def weight_copy(h, way):
        source = w_hbm.at[h, :, span(c, HALF)]
        if shared(h):
            source = w_hbm.at[h, span(odd, HS // 2), span(c, HALF)]
        return remote(
            source, fetched(h, y), w_send.at[h], w_recv.at[h], dy=(ahead, behind)[way]
        )

    def far_copy(h, way):
        part, parts = (odd * 2 + way, 4) if shared(h) else (way, 2)
        ref = weight_ref(h, (behind, ahead)[way], part, parts)
        return remote(ref, ref, far_send.at[h], far_recv.at[h], dy=(ahead, behind)[way])

    def swap_copy(h, owner, send, recv):
        ref = fetched(h, owner)
        return remote(ref, ref, send.at[h], recv.at[h], dx=partner[h])

    def near_side(h, way):
        ref = weight_ref(h, (behind, ahead)[way], 0, 1)
        return remote(ref, ref, near_send.at[h], near_recv.at[h], dc=1 - c)

    def far_side(h):
        ref = weight_ref(h, opposite, 0, 1)
        return remote(ref, ref, side_send.at[h], side_recv.at[h], dc=1 - c)

    def near_rows(h):
        return HS if shared(h) else 2 * HS

    def weight_start(h):
        for way in range(2):
            weight_copy(h, way).start()

    def weight_near(h):
        wait_bytes(weight_bytes(h, near_rows(h)), w_recv.at[h])
        for way in range(2):
            far_copy(h, way).start()
        if shared(h):
            for owner in (behind, ahead):
                swap_copy(h, owner, swap_send, swap_recv).start()
        else:
            for way in range(2):
                near_side(h, way).start()

    def weight_near_swapped(h):
        wait_bytes(weight_bytes(h, HS), swap_recv.at[h])
        for way in range(2):
            near_side(h, way).start()

    def weight_far(h):
        wait_bytes(weight_bytes(h, near_rows(h) // 2), far_recv.at[h])
        if shared(h):
            swap_copy(h, opposite, swap_far_send, swap_far_recv).start()
        else:
            far_side(h).start()

    def weight_far_swapped(h):
        wait_bytes(weight_bytes(h, HS // 2), swap_far_recv.at[h])
        far_side(h).start()

    for h in range(HEADS):
        wait_bytes(kvin.at[h], kv_sem.at[h])
        kv[z, h, c, 0:ROWS, :] = kvin[h, 0]
        turned = kvin[h, 1].T
        kv[z, h, c, ROWS : ROWS + HS, :] = turned[:, :HS]
        kv[z, h, c, ROWS + HS :, :] = turned[:, HS:]
        each_move(z, h, own_plan(h), start)
        if h == 0:
            token_start(2)
        wait_bytes(qin.at[h], q_sem.at[h])
        qt[h, x] = qin[h].T
        for d in (2, 1, 3):
            query_copy(h, d).start()
        weight_start(h)

    attends_copy.wait()
    row = attends[...].astype(F32)
    at_row = lax.broadcasted_iota(jnp.int32, (NZ * NC, GROUPS), 0)
    at_column = lax.broadcasted_iota(jnp.int32, (NZ * NC, GROUPS), 1)
    for place in range(NX):
        group = (at_row // NC) * (NX * NC) + place * NC + at_row % NC
        seen = jnp.sum(jnp.where(at_column == group, row, 0.0), axis=1, keepdims=True)
        bias_out[place] = jnp.broadcast_to(jnp.where(seen > 0.5, 0.0, NONE), (NZ * NC, ROWS))
    bias[x] = bias_out[x]

    def bias_copy(d):
        return remote(bias_out.at[(x + d) % NX], bias.at[x], bias_send, bias_recv, dx=(x + d) % NX)

    for d in range(1, NX):
        bias_copy(d).start()
    own_weight.start()
    gate_copy.start()
    hidden_copy.start()
    acc[...] = jnp.zeros_like(acc)
    top[...] = jnp.full_like(top, NONE)
    total[...] = jnp.zeros_like(total)

    def attend(blocks, h):
        keys = [jnp.concatenate([kv[b, h, s, :ROWS] for s in range(NC)], axis=0) for b in blocks]
        values = [
            jnp.concatenate(
                [kv[b, h, s, ROWS + i * HS : ROWS + i * HS + HS] for s in range(NC) for i in (0, 1)],
                axis=1,
            )
            for b in blocks
        ]
        scores = [
            [jnp.dot(k, qt[h, r], preferred_element_type=F32) for k in keys] for r in range(NX)
        ]
        for r in range(NX):
            parts, offs = [], []
            for i, b in enumerate(blocks):
                for s in range(NC):
                    parts.append(scores[r][i][s * ROWS : (s + 1) * ROWS])
                    offs.append(bias[r, pl.ds(b * NC + s, 1), :])
            old = top[h, r]
            new = old
            for p, o in zip(parts, offs):
                new = jnp.maximum(new, jnp.max(p, axis=0, keepdims=True) + o)
            factor = jnp.exp2((old - new) * SCALE)
            weights = [jnp.exp2(p * SCALE + (o - new * SCALE)) for p, o in zip(parts, offs)]
            top[h, r] = new
            total[h, r] = total[h, r] * factor + sum(
                jnp.sum(w, axis=0, keepdims=True) for w in weights
            )
            rounded = [w.astype(BF16) for w in weights]
            added = sum(
                jnp.dot(
                    v, jnp.concatenate(rounded[NC * i : NC * i + NC], axis=0),
                    preferred_element_type=F32,
                )
                for i, v in enumerate(values)
            )
            acc[h, r] = acc[h, r] * factor + added

    def arrive(step, h):
        for plan in (rising, falling):
            here, b, moves = plan(step, h)

            def take(b=b, moves=moves):
                up_copy(b, h).wait_recv()
                each_move(b, h, moves, start)

            when(here, take)

    def result_copy(h, d):
        return remote(
            osend.at[h, d - 1], orecv.at[h, d - 1], o_send.at[h], o_recv.at[h], dx=(x + d) % NX
        )

    def stats_copy(h, d):
        return remote(
            ssend.at[h, d - 1], srecv.at[h, d - 1], s_send.at[h], s_recv.at[h], dx=(x + d) % NX
        )

    def hand_over(h):
        for d in (2, 1, 3):
            r = (x + d) % NX
            ssend[h, d - 1, 0:1] = top[h, r]
            ssend[h, d - 1, 1:2] = total[h, r]
            stats_copy(h, d).start()
            osend[h, d - 1] = acc[h, r].astype(BF16)
            result_copy(h, d).start()

    def back_copy(h, d):
        dest = (y + d) % NY
        return remote(
            att.at[h, span(dest, PART), :], arecv.at[h, :, span(y, HS)],
            y_send.at[h], y_recv.at[h], dy=dest,
        )

    def merge(h):
        wait_bytes(srecv.at[h], s_recv.at[h])
        wait_bytes(orecv.at[h], o_recv.at[h])
        tops = [top[h, x]] + [srecv[h, d, 0:1] for d in range(NX - 1)]
        totals = [total[h, x]] + [srecv[h, d, 1:2] for d in range(NX - 1)]
        best = functools.reduce(jnp.maximum, tops)
        shares = [jnp.exp2((t - best) * SCALE) for t in tops]
        inverse = 1.0 / sum(s * t for s, t in zip(shares, totals))
        parts = [acc[h, x]] + [orecv[h, d].astype(F32) for d in range(NX - 1)]
        merged = sum(p * (s * inverse) for p, s in zip(parts, shares))
        att[h] = merged.astype(BF16).T
        for d in (2, 1, 3):
            back_copy(h, d).start()
        pltpu.make_async_copy(
            att.at[h, span(y, PART), :], arecv.at[h, :, span(y, HS)], y_recv.at[h]
        ).start()

    def settle(h):
        wait_bytes(qt.at[h, 0 : NX - 1], q_send.at[h])
        each_move(z, h, (z < NZ - 1, (z <= 2) | ((z == 3) & (h == 2)), z >= 0), ended)

        @pl.loop(1, LAST + 1)
        def _(step):
            for plan in (rising, falling):
                _, b, moves = plan(step, h)
                each_move(b, h, moves, ended)

    def pick(i, entries):
        value = jnp.int32(entries[0])
        for at in range(1, len(entries)):
            if entries[at] != entries[at - 1]:
                value = jnp.where(i >= at, entries[at], value)
        return value

    steps, heads = [s for s, _ in ORDER], [h for _, h in ORDER]
    first = [HEADS] + [t + 1 for t in TAKEN[:-1]]
    weight_plan = {
        4: lambda: weight_near(0),
        6: lambda: weight_near(1),
        8: lambda: weight_near_swapped(0),
        9: lambda: weight_near(2),
        11: lambda: (weight_far(0), weight_far(1)),
    }

    @pl.loop(0, len(ORDER))
    def _(i):
        step, h = pick(i, steps), pick(i, heads)

        @pl.loop(pick(i, first), pick(i, TAKEN) + 1)
        def _(j):
            arrive(pick(j, steps), pick(j, heads))

        when(step == 0, lambda: wait_bytes(qt.at[h, 0 : NX - 1], q_recv.at[h]))
        when(i == 0, lambda: wait_bytes(bias.at[0 : NX - 1], bias_recv))

        low = jnp.maximum(z - step, 0)
        high = (z + step) % NZ
        has_low = (z >= step) & reaches_up(low, h, z)
        has_high = (step > 0) & reaches_down(high, h, z) & (high < z)
        when(has_low, lambda: side_copy(low, h, 1 - c).wait_recv())
        when(has_high, lambda: side_copy(high, h, 1 - c).wait_recv())
        when(has_low & has_high, lambda: attend([low, high], h))
        when(has_low != has_high, lambda: attend([jnp.where(has_low, low, high)], h))

        @pl.when(step == LAST)
        def _():
            hand_over(h)
            settle(h)

        for at, act in weight_plan.items():
            when(i == at, act)
        when(i == len(ORDER) - 2, lambda: merge(0))

    weight_far_swapped(0)
    weight_far(2)
    merge(2)
    merge(1)
    for a in range(3):
        wait_bytes(sources[a].at[:, 0 : 3 * HEADS * HS], token_send.at[a])
    wait_bytes(bias.at[0 : NX - 1], bias_send)
    gate_copy.wait()
    hidden_copy.wait()
    own_weight.wait()

    def out_copy(j):
        columns = pl.ds(j * TILE, TILE)
        return pltpu.make_async_copy(out.at[:, columns], out_hbm.at[:, columns], out_sem.at[j])

    for h in range(HEADS):
        wait_bytes(osend.at[h], o_send.at[h])
        wait_bytes(ssend.at[h], s_send.at[h])
        wait_bytes(att.at[h, 0 : 3 * PART], y_send.at[h])
        wait_bytes(weight_bytes(h, near_rows(h)), w_send.at[h])
        wait_bytes(weight_bytes(h, near_rows(h) // 2), far_send.at[h])
        if shared(h):
            wait_bytes(weight_bytes(h, HS), swap_send.at[h])
            wait_bytes(weight_bytes(h, HS // 2), swap_far_send.at[h])
        wait_bytes(weight_bytes(h, 2 * HS), near_send.at[h])
        wait_bytes(weight_bytes(h, HS), side_send.at[h])
    for h in (0, 2, 1):
        wait_bytes(weight_bytes(h, 2 * HS), near_recv.at[h])
        wait_bytes(arecv.at[h], y_recv.at[h])
        wait_bytes(weight_bytes(h, HS), side_recv.at[h])
        for j in range(D // TILE):
            columns = slice(j * TILE, (j + 1) * TILE)
            part = jnp.dot(arecv[h], wbuf[h, :, columns], preferred_element_type=F32)
            if h > 0:
                part = part + summed[:, columns]
            if h != 1:
                summed[:, columns] = part
            else:
                gated = gates[pl.ds(level_ref[0], 1), columns] * part
                out[:, columns] = (hidden[:, columns].astype(F32) + gated).astype(BF16)
                out_copy(j).start()

    for j in range(D // TILE):
        out_copy(j).wait()


def fused(hidden, query, keys, values, attends, levels, weight, gate_table):
    dma = pltpu.SemaphoreType.DMA
    vmem = pltpu.VMEM
    hbm = pl.BlockSpec(memory_space=pltpu.HBM)
    each = dma((HEADS,))
    moving = dma((NZ, HEADS))
    return pl.pallas_call(
        kernel,
        out_shape=jax.ShapeDtypeStruct((PART, D), BF16),
        in_specs=[hbm, hbm, hbm, hbm, hbm, pl.BlockSpec(memory_space=pltpu.SMEM), hbm, hbm],
        out_specs=hbm,
        scratch_shapes=[
            vmem((1, GROUPS), jnp.int32),
            vmem((HEADS, ROWS, HS), BF16),
            vmem((HEADS, 2, ROWS, HS), BF16),
            vmem((NZ, HEADS, NC, 2 * ROWS, HS), BF16),
            vmem((HEADS, NX, HS, ROWS), BF16),
            vmem((NX, NZ * NC, ROWS), F32),
            vmem((NX, NZ * NC, ROWS), F32),
            vmem((HEADS, NX, HS, ROWS), F32),
            vmem((HEADS, NX, 1, ROWS), F32),
            vmem((HEADS, NX, 1, ROWS), F32),
            vmem((HEADS, NX - 1, HS, ROWS), BF16),
            vmem((HEADS, NX - 1, HS, ROWS), BF16),
            vmem((HEADS, NX - 1, 2, ROWS), F32),
            vmem((HEADS, NX - 1, 2, ROWS), F32),
            vmem((HEADS, ROWS, HS), BF16),
            vmem((HEADS, PART, NY * HS), BF16),
            vmem((HEADS, NY * HS, D), BF16),
            vmem((GROUPS, D), F32),
            vmem((PART, D), BF16),
            vmem((PART, D), F32),
            vmem((PART, D), BF16),
            dma((4,)), dma((3,)), each, each, dma(()), dma(()), each, each,
            moving, moving, moving, moving, moving,
            each, each, each, each, each, each,
            each, each, each, each, each, each, each, each,
            each, each, each, each, dma((D // TILE,)),
        ],
        compiler_params=pltpu.CompilerParams(
            collective_id=0, has_side_effects=True, vmem_limit_bytes=60 * 1024 * 1024
        ),
    )(hidden, query, keys, values, attends, levels, weight, gate_table)


def shards(hidden, query, keys, values, attends, levels, out_weight, gate_table):
    weight = out_weight.reshape(HEADS, HS, D)
    return fused(hidden, query, keys, values, attends, levels, weight, gate_table)


def solution(mesh):
    fine = Mesh(mesh.devices.reshape(NZ, NX, NC, NY), ("z", "x", "c", "head"))
    tokens = P(("z", "x", "c", "head"), None)
    group = ("z", "x", "c")
    placed = (
        tokens, tokens, tokens, tokens, P(group, None), P(group), P("head", None), P(),
    )
    return jax.shard_map(
        shards, mesh=fine, in_specs=placed, out_specs=tokens, check_vma=False
    )
```

```python
import functools

import jax
import jax.numpy as jnp
from jax import lax
from jax.experimental import pallas as pl
from jax.experimental.pallas import tpu as pltpu
from jax.sharding import Mesh, PartitionSpec as P

HS = 128
NZ, NX, NC, NY = 8, 4, 2, 4
GROUPS = 64
ROWS = 256
PART = 64
HEADS = 3
D = 3072
HALF = D // NC
TILE = 768
LAST = 4
SCALE = 1.4426950408889634 * HS**-0.5
NONE = -1e30
ORDER = tuple((s, h) for s in range(3) for h in range(3)) + (
    (3, 0), (3, 1), (4, 0), (3, 2), (4, 2), (4, 1),
)
TAKEN = (3, 4, 5, 5, 6, 7, 8, 8, 9, 10, 11, 12, 13, 14, 14)
MESH_ID = pl.DeviceIdType.MESH
F32, BF16 = jnp.float32, jnp.bfloat16


def kernel(
    hidden_hbm, q_hbm, k_hbm, v_hbm, attends_hbm, level_ref, w_hbm, gate_hbm, out_hbm,
    attends, qin, kvin, kv, qt, bias_out, bias, acc, top, total, osend, orecv, ssend, srecv,
    att, arecv, wbuf, gates, hidden, summed, out,
    early_sem, token_send, kv_sem, q_sem, bias_send, bias_recv, q_send, q_recv,
    up_send, dn_send, z_recv, sib_send, sib_recv,
    o_send, o_recv, s_send, s_recv, y_send, y_recv,
    w_send, w_recv, far_send, far_recv, swap_send, swap_recv, swap_far_send, swap_far_recv,
    near_send, near_recv, side_send, side_recv, out_sem,
):
    z, x, c, y = (lax.axis_index(a) for a in ("z", "x", "c", "head"))
    above, below = (z + 1) % NZ, (z + NZ - 1) % NZ

    def remote(src, dst, send, recv, dz=None, dx=None, dc=None, dy=None):
        return pltpu.make_async_remote_copy(
            src_ref=src, dst_ref=dst, send_sem=send, recv_sem=recv,
            device_id=(
                z if dz is None else dz, x if dx is None else dx,
                c if dc is None else dc, y if dy is None else dy,
            ),
            device_id_type=MESH_ID,
        )

    def span(at, size):
        return pl.ds(pl.multiple_of(at * size, size), size)

    def wait_bytes(ref, sem):
        pltpu.make_async_copy(ref, ref, sem).wait()

    attends_copy = pltpu.make_async_copy(attends_hbm, attends, early_sem.at[0])
    own_weight = pltpu.make_async_copy(w_hbm, wbuf.at[:, span(y, HS), :], early_sem.at[1])
    gate_copy = pltpu.make_async_copy(gate_hbm, gates, early_sem.at[2])
    hidden_copy = pltpu.make_async_copy(hidden_hbm, hidden, early_sem.at[3])
    attends_copy.start()

    barrier = pltpu.get_barrier_semaphore()
    peers = [(z, x, c, (y + d) % NY) for d in range(1, NY)]
    peers += [(z, (x + d) % NX, c, y) for d in range(1, NX)]
    peers += [(z, x, 1 - c, y), (above, x, c, y), (below, x, c, y)]
    for peer in peers:
        pl.semaphore_signal(barrier, inc=1, device_id=peer, device_id_type=MESH_ID)
    pl.semaphore_wait(barrier, len(peers))

    sources = [k_hbm, v_hbm, q_hbm]

    def landing(a, h):
        return (kvin.at[h, a] if a < 2 else qin.at[h]).at[span(y, PART), :]

    def landed(a, h):
        return (kv_sem if a < 2 else q_sem).at[h]

    def token_copy(a, h, d):
        dest = (y + d) % NY
        return remote(
            sources[a].at[:, span(dest * HEADS + h, HS)], landing(a, h),
            token_send.at[a], landed(a, h), dy=dest,
        )

    def token_start(a, h):
        for d in (2, 1, 3):
            token_copy(a, h, d).start()
        pltpu.make_async_copy(
            sources[a].at[:, span(y * HEADS + h, HS)], landing(a, h), landed(a, h)
        ).start()

    for a, h in ((0, 0), (1, 0), (2, 0), (2, 1), (0, 1), (1, 1), (2, 2), (0, 2), (1, 2)):
        token_start(a, h)

    def up_copy(b, h):
        ref = kv.at[b, h, c]
        return remote(ref, ref, up_send.at[b, h], z_recv.at[b, h], dz=above)

    def down_copy(b, h):
        ref = kv.at[b, h, c]
        return remote(ref, ref, dn_send.at[b, h], z_recv.at[b, h], dz=below)

    def side_copy(b, h, side):
        ref = kv.at[b, h, side]
        return remote(ref, ref, sib_send.at[b, h], sib_recv.at[b, h], dc=1 - c)

    def reaches_up(b, h, plane):
        return (plane < NZ) & ((plane - b <= 3) | ((plane == NZ - 1) & (b == 3) & (h < 2)))

    def reaches_down(b, h, plane):
        return ((b <= 2) & ((plane >= b + 4) | (plane < b))) | (
            (b == 3) & (h == 2) & ((plane == NZ - 1) | (plane < b))
        )

    def when(condition, act):
        @pl.when(condition)
        def _():
            act()

    def each_move(b, h, moves, act):
        up, down, side = moves
        if up is not None:
            when(up, lambda: act(up_copy(b, h)))
        if down is not None:
            when(down, lambda: act(down_copy(b, h)))
        when(side, lambda: act(side_copy(b, h, c)))

    def start(copy):
        copy.start()

    def ended(copy):
        copy.wait_send()

    def own_plan(h):
        return z < NZ - 1, z <= (3 if h == 2 else 2), z >= 0

    def rising(step, h):
        b = jnp.maximum(z - step, 0)
        here = (z >= step) & reaches_up(b, h, z)
        return here, b, (here & reaches_up(b, h, z + 1), None, here)

    def falling(step, h):
        b = (z + step) % NZ
        here = reaches_down(b, h, z)
        return here, b, (None, here & reaches_down(b, h, below), here & (b < z))

    def query_copy(h, d):
        return remote(qt.at[h, x], qt.at[h, x], q_send.at[h], q_recv.at[h], dx=(x + d) % NX)

    ahead, behind, opposite = (y + 1) % NY, (y + NY - 1) % NY, (y + 2) % NY

    odd = x % 2
    partner = ((x + 1 - 2 * odd) % NX, (x + NX - 1 + 2 * odd) % NX)

    def weight_ref(h, owner, part, parts):
        size = HS // parts
        rows = pl.ds(pl.multiple_of(owner * HS + part * size, size), size)
        return wbuf.at[h, rows, span(c, HALF)]

    def weight_bytes(h, rows):
        return wbuf.at[h, 0:rows, 0:HALF]

    def shared(h):
        return h < 1

    def fetched(h, owner):
        return weight_ref(h, owner, odd, 2) if shared(h) else weight_ref(h, owner, 0, 1)

    def weight_copy(h, way):
        source = w_hbm.at[h, :, span(c, HALF)]
        if shared(h):
            source = w_hbm.at[h, span(odd, HS // 2), span(c, HALF)]
        return remote(
            source, fetched(h, y), w_send.at[h], w_recv.at[h], dy=(ahead, behind)[way]
        )

    def far_copy(h, way):
        part, parts = (odd * 2 + way, 4) if shared(h) else (way, 2)
        ref = weight_ref(h, (behind, ahead)[way], part, parts)
        return remote(ref, ref, far_send.at[h], far_recv.at[h], dy=(ahead, behind)[way])

    def swap_copy(h, owner, send, recv):
        ref = fetched(h, owner)
        return remote(ref, ref, send.at[h], recv.at[h], dx=partner[h])

    def near_side(h, way):
        ref = weight_ref(h, (behind, ahead)[way], 0, 1)
        return remote(ref, ref, near_send.at[h], near_recv.at[h], dc=1 - c)

    def far_side(h):
        ref = weight_ref(h, opposite, 0, 1)
        return remote(ref, ref, side_send.at[h], side_recv.at[h], dc=1 - c)

    def near_rows(h):
        return HS if shared(h) else 2 * HS

    def weight_start(h):
        for way in range(2):
            weight_copy(h, way).start()

    def weight_near(h):
        wait_bytes(weight_bytes(h, near_rows(h)), w_recv.at[h])
        for way in range(2):
            far_copy(h, way).start()
        if shared(h):
            for owner in (behind, ahead):
                swap_copy(h, owner, swap_send, swap_recv).start()
        else:
            for way in range(2):
                near_side(h, way).start()

    def weight_near_swapped(h):
        wait_bytes(weight_bytes(h, HS), swap_recv.at[h])
        for way in range(2):
            near_side(h, way).start()

    def weight_far(h):
        wait_bytes(weight_bytes(h, near_rows(h) // 2), far_recv.at[h])
        if shared(h):
            swap_copy(h, opposite, swap_far_send, swap_far_recv).start()
        else:
            far_side(h).start()

    def weight_far_swapped(h):
        wait_bytes(weight_bytes(h, HS // 2), swap_far_recv.at[h])
        far_side(h).start()

    def own_block(h):
        wait_bytes(kvin.at[h], kv_sem.at[h])
        kv[z, h, c, 0:ROWS, :] = kvin[h, 0]
        turned = kvin[h, 1].T
        kv[z, h, c, ROWS : ROWS + HS, :] = turned[:, :HS]
        kv[z, h, c, ROWS + HS :, :] = turned[:, HS:]
        each_move(z, h, own_plan(h), start)

    def own_query(h):
        wait_bytes(qin.at[h], q_sem.at[h])
        qt[h, x] = qin[h].T
        for d in (2, 1, 3):
            query_copy(h, d).start()

    own_block(0)
    own_query(0)
    own_query(1)
    own_block(1)
    own_query(2)
    own_block(2)
    for h in range(HEADS):
        weight_start(h)

    attends_copy.wait()
    row = attends[...].astype(F32)
    at_row = lax.broadcasted_iota(jnp.int32, (NZ * NC, GROUPS), 0)
    at_column = lax.broadcasted_iota(jnp.int32, (NZ * NC, GROUPS), 1)
    for place in range(NX):
        group = (at_row // NC) * (NX * NC) + place * NC + at_row % NC
        seen = jnp.sum(jnp.where(at_column == group, row, 0.0), axis=1, keepdims=True)
        bias_out[place] = jnp.broadcast_to(jnp.where(seen > 0.5, 0.0, NONE), (NZ * NC, ROWS))
    bias[x] = bias_out[x]

    def bias_copy(d):
        return remote(bias_out.at[(x + d) % NX], bias.at[x], bias_send, bias_recv, dx=(x + d) % NX)

    for d in range(1, NX):
        bias_copy(d).start()
    own_weight.start()
    gate_copy.start()
    hidden_copy.start()
    acc[...] = jnp.zeros_like(acc)
    top[...] = jnp.full_like(top, NONE)
    total[...] = jnp.zeros_like(total)

    def attend(blocks, h):
        keys = [jnp.concatenate([kv[b, h, s, :ROWS] for s in range(NC)], axis=0) for b in blocks]
        values = [
            jnp.concatenate(
                [kv[b, h, s, ROWS + i * HS : ROWS + i * HS + HS] for s in range(NC) for i in (0, 1)],
                axis=1,
            )
            for b in blocks
        ]
        scores = [
            [jnp.dot(k, qt[h, r], preferred_element_type=F32) for k in keys] for r in range(NX)
        ]
        for r in range(NX):
            parts, offs = [], []
            for i, b in enumerate(blocks):
                for s in range(NC):
                    parts.append(scores[r][i][s * ROWS : (s + 1) * ROWS])
                    offs.append(bias[r, pl.ds(b * NC + s, 1), :])
            old = top[h, r]
            new = old
            for p, o in zip(parts, offs):
                new = jnp.maximum(new, jnp.max(p, axis=0, keepdims=True) + o)
            factor = jnp.exp2((old - new) * SCALE)
            weights = [jnp.exp2(p * SCALE + (o - new * SCALE)) for p, o in zip(parts, offs)]
            top[h, r] = new
            total[h, r] = total[h, r] * factor + sum(
                jnp.sum(w, axis=0, keepdims=True) for w in weights
            )
            rounded = [w.astype(BF16) for w in weights]
            added = sum(
                jnp.dot(
                    v, jnp.concatenate(rounded[NC * i : NC * i + NC], axis=0),
                    preferred_element_type=F32,
                )
                for i, v in enumerate(values)
            )
            acc[h, r] = acc[h, r] * factor + added

    def arrive(step, h):
        for plan in (rising, falling):
            here, b, moves = plan(step, h)

            def take(b=b, moves=moves):
                up_copy(b, h).wait_recv()
                each_move(b, h, moves, start)

            when(here, take)

    def result_copy(h, d):
        return remote(
            osend.at[h, d - 1], orecv.at[h, d - 1], o_send.at[h], o_recv.at[h], dx=(x + d) % NX
        )

    def stats_copy(h, d):
        return remote(
            ssend.at[h, d - 1], srecv.at[h, d - 1], s_send.at[h], s_recv.at[h], dx=(x + d) % NX
        )

    def hand_over(h):
        for d in (2, 1, 3):
            r = (x + d) % NX
            ssend[h, d - 1, 0:1] = top[h, r]
            ssend[h, d - 1, 1:2] = total[h, r]
            stats_copy(h, d).start()
            osend[h, d - 1] = acc[h, r].astype(BF16)
            result_copy(h, d).start()

    def back_copy(h, d):
        dest = (y + d) % NY
        return remote(
            att.at[h, span(dest, PART), :], arecv.at[h, :, span(y, HS)],
            y_send.at[h], y_recv.at[h], dy=dest,
        )

    def merge(h):
        wait_bytes(srecv.at[h], s_recv.at[h])
        wait_bytes(orecv.at[h], o_recv.at[h])
        tops = [top[h, x]] + [srecv[h, d, 0:1] for d in range(NX - 1)]
        totals = [total[h, x]] + [srecv[h, d, 1:2] for d in range(NX - 1)]
        best = functools.reduce(jnp.maximum, tops)
        shares = [jnp.exp2((t - best) * SCALE) for t in tops]
        inverse = 1.0 / sum(s * t for s, t in zip(shares, totals))
        parts = [acc[h, x]] + [orecv[h, d].astype(F32) for d in range(NX - 1)]
        merged = sum(p * (s * inverse) for p, s in zip(parts, shares))
        att[h] = merged.astype(BF16).T
        for d in (2, 1, 3):
            back_copy(h, d).start()
        pltpu.make_async_copy(
            att.at[h, span(y, PART), :], arecv.at[h, :, span(y, HS)], y_recv.at[h]
        ).start()

    def settle(h):
        wait_bytes(qt.at[h, 0 : NX - 1], q_send.at[h])
        each_move(z, h, (z < NZ - 1, (z <= 2) | ((z == 3) & (h == 2)), z >= 0), ended)

        @pl.loop(1, LAST + 1)
        def _(step):
            for plan in (rising, falling):
                _, b, moves = plan(step, h)
                each_move(b, h, moves, ended)

    def pick(i, entries):
        value = jnp.int32(entries[0])
        for at in range(1, len(entries)):
            if entries[at] != entries[at - 1]:
                value = jnp.where(i >= at, entries[at], value)
        return value

    steps, heads = [s for s, _ in ORDER], [h for _, h in ORDER]
    first = [HEADS] + [t + 1 for t in TAKEN[:-1]]
    weight_plan = {
        4: lambda: weight_near(0),
        6: lambda: weight_near(1),
        8: lambda: weight_near_swapped(0),
        9: lambda: weight_near(2),
        11: lambda: (weight_far(0), weight_far(1)),
    }

    @pl.loop(0, len(ORDER))
    def _(i):
        step, h = pick(i, steps), pick(i, heads)

        @pl.loop(pick(i, first), pick(i, TAKEN) + 1)
        def _(j):
            arrive(pick(j, steps), pick(j, heads))

        when(step == 0, lambda: wait_bytes(qt.at[h, 0 : NX - 1], q_recv.at[h]))
        when(i == 0, lambda: wait_bytes(bias.at[0 : NX - 1], bias_recv))

        low = jnp.maximum(z - step, 0)
        high = (z + step) % NZ
        has_low = (z >= step) & reaches_up(low, h, z)
        has_high = (step > 0) & reaches_down(high, h, z) & (high < z)
        when(has_low, lambda: side_copy(low, h, 1 - c).wait_recv())
        when(has_high, lambda: side_copy(high, h, 1 - c).wait_recv())
        when(has_low & has_high, lambda: attend([low, high], h))
        when(has_low != has_high, lambda: attend([jnp.where(has_low, low, high)], h))

        @pl.when(step == LAST)
        def _():
            hand_over(h)

        for at, act in weight_plan.items():
            when(i == at, act)
        when(i == len(ORDER) - 2, lambda: merge(0))

    weight_far_swapped(0)
    weight_far(2)
    merge(2)
    merge(1)
    for a in range(3):
        wait_bytes(sources[a].at[:, 0 : 3 * HEADS * HS], token_send.at[a])
    wait_bytes(bias.at[0 : NX - 1], bias_send)
    gate_copy.wait()
    hidden_copy.wait()
    own_weight.wait()

    def out_copy(j):
        columns = pl.ds(j * TILE, TILE)
        return pltpu.make_async_copy(out.at[:, columns], out_hbm.at[:, columns], out_sem.at[j])

    for h in range(HEADS):
        settle(h)
    for h in range(HEADS):
        wait_bytes(osend.at[h], o_send.at[h])
        wait_bytes(ssend.at[h], s_send.at[h])
        wait_bytes(att.at[h, 0 : 3 * PART], y_send.at[h])
        wait_bytes(weight_bytes(h, near_rows(h)), w_send.at[h])
        wait_bytes(weight_bytes(h, near_rows(h) // 2), far_send.at[h])
        if shared(h):
            wait_bytes(weight_bytes(h, HS), swap_send.at[h])
            wait_bytes(weight_bytes(h, HS // 2), swap_far_send.at[h])
        wait_bytes(weight_bytes(h, 2 * HS), near_send.at[h])
        wait_bytes(weight_bytes(h, HS), side_send.at[h])
    for h in (0, 2, 1):
        wait_bytes(weight_bytes(h, 2 * HS), near_recv.at[h])
        wait_bytes(arecv.at[h], y_recv.at[h])
        wait_bytes(weight_bytes(h, HS), side_recv.at[h])
        for j in range(D // TILE):
            columns = slice(j * TILE, (j + 1) * TILE)
            part = jnp.dot(arecv[h], wbuf[h, :, columns], preferred_element_type=F32)
            if h > 0:
                part = part + summed[:, columns]
            if h != 1:
                summed[:, columns] = part
            else:
                gated = gates[pl.ds(level_ref[0], 1), columns] * part
                out[:, columns] = (hidden[:, columns].astype(F32) + gated).astype(BF16)
                out_copy(j).start()

    for j in range(D // TILE):
        out_copy(j).wait()


def fused(hidden, query, keys, values, attends, levels, weight, gate_table):
    dma = pltpu.SemaphoreType.DMA
    vmem = pltpu.VMEM
    hbm = pl.BlockSpec(memory_space=pltpu.HBM)
    each = dma((HEADS,))
    moving = dma((NZ, HEADS))
    return pl.pallas_call(
        kernel,
        out_shape=jax.ShapeDtypeStruct((PART, D), BF16),
        in_specs=[hbm, hbm, hbm, hbm, hbm, pl.BlockSpec(memory_space=pltpu.SMEM), hbm, hbm],
        out_specs=hbm,
        scratch_shapes=[
            vmem((1, GROUPS), jnp.int32),
            vmem((HEADS, ROWS, HS), BF16),
            vmem((HEADS, 2, ROWS, HS), BF16),
            vmem((NZ, HEADS, NC, 2 * ROWS, HS), BF16),
            vmem((HEADS, NX, HS, ROWS), BF16),
            vmem((NX, NZ * NC, ROWS), F32),
            vmem((NX, NZ * NC, ROWS), F32),
            vmem((HEADS, NX, HS, ROWS), F32),
            vmem((HEADS, NX, 1, ROWS), F32),
            vmem((HEADS, NX, 1, ROWS), F32),
            vmem((HEADS, NX - 1, HS, ROWS), BF16),
            vmem((HEADS, NX - 1, HS, ROWS), BF16),
            vmem((HEADS, NX - 1, 2, ROWS), F32),
            vmem((HEADS, NX - 1, 2, ROWS), F32),
            vmem((HEADS, ROWS, HS), BF16),
            vmem((HEADS, PART, NY * HS), BF16),
            vmem((HEADS, NY * HS, D), BF16),
            vmem((GROUPS, D), F32),
            vmem((PART, D), BF16),
            vmem((PART, D), F32),
            vmem((PART, D), BF16),
            dma((4,)), dma((3,)), each, each, dma(()), dma(()), each, each,
            moving, moving, moving, moving, moving,
            each, each, each, each, each, each,
            each, each, each, each, each, each, each, each,
            each, each, each, each, dma((D // TILE,)),
        ],
        compiler_params=pltpu.CompilerParams(
            collective_id=0, has_side_effects=True, vmem_limit_bytes=60 * 1024 * 1024
        ),
    )(hidden, query, keys, values, attends, levels, weight, gate_table)


def shards(hidden, query, keys, values, attends, levels, out_weight, gate_table):
    weight = out_weight.reshape(HEADS, HS, D)
    return fused(hidden, query, keys, values, attends, levels, weight, gate_table)


def solution(mesh):
    fine = Mesh(mesh.devices.reshape(NZ, NX, NC, NY), ("z", "x", "c", "head"))
    tokens = P(("z", "x", "c", "head"), None)
    group = ("z", "x", "c")
    placed = (
        tokens, tokens, tokens, tokens, P(group, None), P(group), P("head", None), P(),
    )
    return jax.shard_map(
        shards, mesh=fine, in_specs=placed, out_specs=tokens, check_vma=False
    )
```
